256 devices in a mesh: band: 32 (over y_hi, z, core), pw: 8 (over y_lo, x).
Axes of the slice: x: 4, y: 4 (y_hi: 2, y_lo: 2; y = y_hi * 2 + y_lo), z: 8, core: 2. Of those that a mesh axis runs over, the one named last changes fastest.
Arguments:
- orbitals: float32 [64, 128, 128, 128], P('band', 'pw'), may hold values from -6 to 6
- occupations: int32 [64], P('band'), may hold values from 1 to 2
Outputs:
- exchange_out: float32 [64, 128, 128, 128], P('band', 'pw')
The draws below stay inside these ranges and needn't reach their ends.
All inputs are finite; a program needn't handle non-finite values.
Results may differ from the reference program's by a relative error of at most 0.000084.
Values sent between devices are 32-bit elements; how exact they have to be, the bound alone decides.
A program may use at most 128 MiB of HBM per device.

```python
import jax
import jax.numpy as jnp
from jax import lax

NX = 128
NY = 128
NZ = 128
BANDS_DEV = 2
BANDS = 64
N_BAND = 32


def with_ends(array, own_key, least, largest):
    longest = array.shape.index(max(array.shape))
    spots = []
    for shift in (0, 1):
        where = [jax.random.randint(jax.random.fold_in(own_key, axis), (), 0, length) for axis, length in enumerate(array.shape)]
        where[longest] = (where[longest] + shift) % array.shape[longest]
        spots.append(tuple(where))
    return array.at[spots[0]].set(least).at[spots[1]].set(largest)


def levels(rng, shape, split, smallest, top_value):
    level = 1.0
    for position, parts in split:
        heights = jax.random.uniform(jax.random.fold_in(jax.random.fold_in(rng, 6), position), (parts,), jnp.float32, smallest / len(split), top_value / len(split))
        level = level * jnp.repeat(jnp.exp(heights), shape[position] // parts).reshape((-1,) + (1,) * (len(shape) - 1 - position))
    return level


def centred(own_key, extent, scale, most, pieces=(), kind=jnp.bfloat16):
    result = jax.random.normal(own_key, extent, jnp.float32) * scale
    if len(pieces) > 0:
        result = levels(own_key, extent, pieces, -0.22, 0.18) * result
    return jnp.clip(result, min=-most, max=most).astype(kind)


def setup_inputs(seed: int = 0) -> dict:
    streams_of = jax.random.split(jax.random.key(seed), 3)
    orbitals = centred(streams_of[0], (BANDS, NX, NY, NZ), 1.0, 6.0, ((0, 32), (1, 8)), jnp.float32)
    occupations = with_ends(jax.random.randint(streams_of[1], (BANDS,), 1, 3), jax.random.fold_in(streams_of[1], 1), 1, 2).astype(jnp.int32)
    return {"orbitals": orbitals, "occupations": occupations}


MIXING = 0.25


def wave_numbers(length):
    index = jnp.arange(length, dtype=jnp.int32)
    signed = jnp.where(index < length // 2, index, index - length)
    return signed.astype(jnp.float32) * (2.0 * jnp.pi / length)


def coulomb_table():
    wave_x = wave_numbers(NX)
    wave_y = wave_numbers(NY)
    wave_z = wave_numbers(NZ)
    square = wave_x[:, None, None] * wave_x[:, None, None] + wave_y[None, :, None] * wave_y[None, :, None] + wave_z[None, None, :] * wave_z[None, None, :]
    safe = jnp.where(square > 0, square, 1.0)
    return jnp.where(square > 0, 4.0 * jnp.pi / safe, 0.0)


def reference(orbitals, occupations):
    groups = N_BAND
    blocks = orbitals.reshape((groups, BANDS_DEV, NX, NY, NZ))
    weights = (occupations.astype(jnp.float32) * 0.5).reshape((groups, BANDS_DEV))
    previous = jnp.roll(blocks, 1, axis=0)
    previous_weights = jnp.roll(weights, 1, axis=0)
    coulomb = coulomb_table()

    def one_group(items):
        resident, passing, resident_weights, passing_weights = items
        densities = resident[:, None] * passing[None, :]
        spectrum = jnp.fft.fftn(densities, axes=(2, 3, 4)) * coulomb
        potential = jnp.real(jnp.fft.ifftn(spectrum, axes=(2, 3, 4)))
        own = -MIXING * jnp.sum(potential * (passing_weights[:, None, None, None] * passing)[None], axis=1)
        theirs = -MIXING * jnp.sum(potential * (resident_weights[:, None, None, None] * resident)[:, None], axis=0)
        return own, theirs

    own, theirs = lax.map(one_group, (blocks, previous, weights, previous_weights))
    total = own + jnp.roll(theirs, -1, axis=0)
    return total.reshape((BANDS, NX, NY, NZ))
```

```python
import jax
import jax.numpy as jnp
import numpy as np
from jax import lax
from jax.sharding import PartitionSpec as P

MIXING = 0.25


def passed_along(value, axis, steps):
    count = lax.axis_size(axis)
    pairs = [(source, (source + steps) % count) for source in range(count)]
    return lax.ppermute(value, axis, pairs)


def basis(length):
    half = length // 2
    grid = np.arange(length)
    columns, waves = [], []
    for k in range(half + 1):
        scale = np.sqrt((1.0 if k in (0, half) else 2.0) / length)
        columns.append(scale * np.cos(2.0 * np.pi * (k * grid % length) / length))
        waves.append(k)
    for k in range(1, half):
        scale = np.sqrt(2.0 / length)
        columns.append(scale * np.sin(2.0 * np.pi * (k * grid % length) / length))
        waves.append(k)
    return np.stack(columns, axis=1).astype(np.float32), np.array(waves)


def apply_table(form, field, table):
    return jnp.einsum(form, field, table, precision=lax.Precision.HIGH)


def shards(orbitals, occupations):
    count = orbitals.shape[0]
    slab_x, full_y, full_z = (orbitals.shape[1], orbitals.shape[2], orbitals.shape[3])
    groups = lax.axis_size("pw")
    full_x = slab_x * groups
    slab_y = full_y // groups
    table_x, waves_x = basis(full_x)
    table_y, waves_y = basis(full_y)
    table_z, waves_z = basis(full_z)
    weights = occupations.astype(jnp.float32) * 0.5
    passing, passing_weights = passed_along((orbitals, weights), "band", 1)
    densities = (orbitals[:, None] * passing[None, :]).reshape(
        (count * count, slab_x, full_y, full_z)
    )
    field = apply_table("pxyn,nk->pxyk", densities, table_z)
    field = apply_table("pxny,nk->pxky", field, table_y)
    start_y = lax.axis_index("pw") * slab_y
    wave_x = jnp.asarray(waves_x * (2.0 * np.pi / full_x), jnp.float32)
    wave_y = lax.dynamic_slice_in_dim(
        jnp.asarray(waves_y * (2.0 * np.pi / full_y), jnp.float32), start_y, slab_y
    )
    wave_z = jnp.asarray(waves_z * (2.0 * np.pi / full_z), jnp.float32)
    square = (
        wave_x[:, None, None] * wave_x[:, None, None]
        + wave_y[None, :, None] * wave_y[None, :, None]
        + wave_z[None, None, :] * wave_z[None, None, :]
    )
    safe = jnp.where(square > 0, square, 1.0)
    coulomb = jnp.where(square > 0, 4.0 * jnp.pi / safe, 0.0)
    field = lax.all_to_all(field, "pw", split_axis=2, concat_axis=1, tiled=True)
    spectrum = apply_table("pnyz,nk->pkyz", field, table_x) * coulomb
    field = apply_table("pkyz,nk->pnyz", spectrum, table_x)
    field = lax.all_to_all(field, "pw", split_axis=1, concat_axis=2, tiled=True)
    field = apply_table("pxky,nk->pxny", field, table_y)
    potential = apply_table("pxyk,nk->pxyn", field, table_z)
    potential = potential.reshape((count, count, slab_x, full_y, full_z))
    theirs = jnp.sum(
        potential * ((-MIXING * weights)[:, None, None, None] * orbitals)[:, None], axis=0
    )
    returned = passed_along(theirs, "band", -1)
    own = jnp.sum(
        potential * ((-MIXING * passing_weights)[:, None, None, None] * passing)[None], axis=1
    )
    return own + returned


def solution(mesh):
    placed = (P("band", "pw", None, None), P("band"))
    return jax.shard_map(
        shards, mesh=mesh, in_specs=placed, out_specs=P("band", "pw", None, None), check_vma=False
    )
```

```python
import functools

import jax
import jax.numpy as jnp
import numpy as np
from jax import lax
from jax.experimental import pallas as pl
from jax.experimental.pallas import tpu as pltpu
from jax.sharding import PartitionSpec as P

MIXING = 0.25
N = 128
HALF = N // 2
SLAB = 16
HALVES = 2
ROWS = SLAB // HALVES
MESH = pl.DeviceIdType.MESH
FAR_FIRST = ((2, 1), (2, 0), (1, 1), (3, 1), (0, 1), (1, 0), (3, 0))
PAIRS = ((0, 0), (1, 0), (0, 1), (1, 1))


def tables():
    grid = np.arange(N)
    cosines = [np.cos(2.0 * np.pi * (k * grid % N) / N) for k in range(HALF + 1)]
    sines = [np.sin(2.0 * np.pi * (k * grid % N) / N) for k in range(1, HALF)]
    table = np.stack(cosines + sines, axis=1).astype(np.float32)
    high = table.astype(jnp.bfloat16)
    low = (table - high.astype(np.float32)).astype(jnp.bfloat16)
    right_forward = np.block([[high, low], [high, low]])
    left_forward = np.block([[high.T, high.T], [low.T, low.T]])
    left_inverse = np.block([[high, high], [low, low]])
    right_inverse = np.block([[high.T, low.T], [high.T, low.T]])
    return np.stack([right_forward, left_forward, left_inverse, right_inverse])


def split(value):
    high = value.astype(jnp.bfloat16)
    low = (value - high.astype(jnp.float32)).astype(jnp.bfloat16)
    return high, low


def from_right(value, table):
    high, low = split(value)
    both = jnp.dot(
        jnp.concatenate([high, low], axis=1), table, preferred_element_type=jnp.float32
    )
    return both[:, :N] + both[:, N:]


def from_left(table, value):
    high, low = split(value)
    both = jnp.dot(
        table, jnp.concatenate([high, low], axis=0), preferred_element_type=jnp.float32
    )
    return both[:N] + both[N:]


def side_by_side(value):
    return jnp.concatenate([value[:N], value[N:]], axis=1)


def stacked(value):
    return jnp.concatenate([value[:, :N], value[:, N:]], axis=0)


def wave_numbers(index):
    wave = jnp.where(index > HALF, index - HALF, index)
    share = jnp.where((wave == 0) | (wave == HALF), 1.0 / N, 2.0 / N)
    wave = wave.astype(jnp.float32) * (2.0 * np.pi / N)
    return wave * wave, share


def kernel(
    occupations, orbitals, table, out, passing, weights, passed_weights, sent, middle, back,
    theirs, returned, coulomb, turned, pass_send, pass_recv, weight_send, weight_recv, go_send,
    go_recv, come_send, come_recv, term_send, term_recv, local_sem,
):
    band = lax.axis_index("band")
    place = lax.axis_index("pw")
    bands = lax.axis_size("band")
    following = {"band": lax.rem(band + 1, bands)}
    previous = {"band": lax.rem(band + bands - 1, bands)}
    place_x, place_y = lax.rem(place, 4), lax.div(place, 4)
    peers = [
        lax.rem(place_y + dy, 2) * 4 + lax.rem(place_x + dx, 4) for dx, dy in FAR_FIRST
    ]

    for i in range(2):
        weight = occupations[i].astype(jnp.float32) * (-0.5 * MIXING)
        weights[i] = jnp.full((8, N), weight, jnp.float32)

    barrier = pltpu.get_barrier_semaphore()
    for device in [following, previous] + [{"pw": peer} for peer in peers]:
        pl.semaphore_signal(barrier, inc=1, device_id=device, device_id_type=MESH)
    pl.semaphore_wait(barrier, 2 + len(peers))

    passes = [
        pltpu.make_async_remote_copy(
            src_ref=orbitals.at[j], dst_ref=passing.at[j], send_sem=pass_send.at[j],
            recv_sem=pass_recv.at[j], device_id=following, device_id_type=MESH,
        )
        for j in range(2)
    ]
    weight_pass = pltpu.make_async_remote_copy(
        src_ref=weights, dst_ref=passed_weights, send_sem=weight_send, recv_sem=weight_recv,
        device_id=following, device_id_type=MESH,
    )
    passes[0].start()
    weight_pass.start()
    passes[1].start()

    def slab(index):
        return pl.ds(pl.multiple_of(index * SLAB, SLAB), SLAB)

    goes, comes, stays = [], [], []
    for p in range(4):
        goes.append([
            pltpu.make_async_remote_copy(
                src_ref=sent.at[p, slab(peer)], dst_ref=middle.at[p, :, slab(place)],
                send_sem=go_send.at[p, n], recv_sem=go_recv.at[p, n],
                device_id={"pw": peer}, device_id_type=MESH,
            )
            for n, peer in enumerate(peers)
        ])
        comes.append([
            pltpu.make_async_remote_copy(
                src_ref=middle.at[p, :, slab(peer)], dst_ref=back.at[p, slab(place)],
                send_sem=come_send.at[p, n], recv_sem=come_recv.at[p, n],
                device_id={"pw": peer}, device_id_type=MESH,
            )
            for n, peer in enumerate(peers)
        ])
        stays.append((
            pltpu.make_async_copy(
                sent.at[p, slab(place)], middle.at[p, :, slab(place)], local_sem.at[p, 0]
            ),
            pltpu.make_async_copy(
                middle.at[p, :, slab(place)], back.at[p, slab(place)], local_sem.at[p, 1]
            ),
        ))
    terms = [
        [
            pltpu.make_async_remote_copy(
                src_ref=theirs.at[j, pl.ds(h * ROWS, ROWS)],
                dst_ref=returned.at[j, pl.ds(h * ROWS, ROWS)],
                send_sem=term_send.at[j, h], recv_sem=term_recv.at[j, h],
                device_id=previous, device_id_type=MESH,
            )
            for h in range(HALVES)
        ]
        for j in range(2)
    ]

    for p, (i, j) in enumerate(PAIRS):
        if i == 0:
            passes[j].wait_recv()

        @pl.loop(0, HALVES)
        def _(h):
            @pl.loop(0, ROWS // 4)
            def _(quad):
                for r in range(2):
                    at = pl.ds(h * ROWS + quad * 4 + r * 2, 2)
                    field = (orbitals[i, at] * passing[j, at]).reshape(2 * N, N)
                    field = from_right(field, table[0])
                    field = from_left(table[1], side_by_side(field))
                    turned[quad * 4 + r * 2] = field[:, :N]
                    turned[quad * 4 + r * 2 + 1] = field[:, N:]

            @pl.loop(0, N // 16)
            def _(block):
                for b in range(2):
                    rows = pl.ds(pl.multiple_of(block * 16 + b * 8, 8), 8)
                    sent[p, rows, pl.ds(pl.multiple_of(h * ROWS, ROWS), ROWS)] = jnp.swapaxes(
                        turned[:, rows], 0, 1
                    )

        stays[p][0].start()
        for copy in goes[p]:
            copy.start()
        if p == 1:
            wave_x, share_x = wave_numbers(lax.broadcasted_iota(jnp.int32, (N, N), 0))
            wave_z, share_z = wave_numbers(lax.broadcasted_iota(jnp.int32, (N, N), 1))
            square_xz = wave_x + wave_z
            share_xz = share_x * share_z

            @pl.loop(0, SLAB)
            def _(y):
                wave_y, share_y = wave_numbers(
                    jnp.full((N, N), place * SLAB + y, jnp.int32)
                )
                square = square_xz + wave_y
                safe = jnp.where(square > 0, square, 1.0)
                factor = (4.0 * np.pi) * (share_xz * share_y)
                coulomb[y] = jnp.where(square > 0, factor / safe, 0.0)

    for p in range(4):
        stays[p][0].wait()
        for copy in goes[p]:
            copy.wait_recv()

        @pl.loop(0, SLAB // 4)
        def _(quad):
            for r in range(2):
                y = quad * 4 + r * 2
                field = jnp.concatenate([middle[p, y], middle[p, y + 1]], axis=1)
                field = from_left(table[1], field)
                field = field * jnp.concatenate([coulomb[y], coulomb[y + 1]], axis=1)
                field = from_left(table[2], field)
                middle[p, y] = field[:, :N]
                middle[p, y + 1] = field[:, N:]

        stays[p][1].start()
        for copy in comes[p]:
            copy.start()

    weight_pass.wait_recv()
    for p, (i, j) in enumerate(PAIRS):
        stays[p][1].wait()
        for copy in comes[p]:
            copy.wait_recv()
        for h in range(HALVES):

            @pl.loop(0, N // 16)
            def _(block):
                for b in range(2):
                    rows = pl.ds(pl.multiple_of(block * 16 + b * 8, 8), 8)
                    turned[:, rows] = jnp.swapaxes(back[p, rows, h * ROWS : (h + 1) * ROWS], 0, 1)

            @pl.loop(0, ROWS // 4)
            def _(quad):
                for r in range(2):
                    y = quad * 4 + r * 2
                    field = jnp.concatenate([turned[y], turned[y + 1]], axis=1)
                    field = from_left(table[2], field)
                    field = from_right(stacked(field), table[3])
                    potential = field.reshape(2, N // 8, 8, N)
                    at = pl.ds(h * ROWS + y, 2)
                    mine = (
                        potential * passing[j, at].reshape(2, N // 8, 8, N) * passed_weights[j]
                    ).reshape(2, N, N)
                    other = (
                        potential * orbitals[i, at].reshape(2, N // 8, 8, N) * weights[i]
                    ).reshape(2, N, N)
                    if j == 0:
                        out[i, at] = mine
                    else:
                        out[i, at] += mine
                    if i == 0:
                        theirs[j, at] = other
                    else:
                        theirs[j, at] += other

            if i == 1:
                terms[j][h].start()

    for j in range(2):
        for h in range(HALVES):
            terms[j][h].wait_recv()

            @pl.loop(0, ROWS)
            def _(row):
                out[j, h * ROWS + row] += returned[j, h * ROWS + row]

    for copy in passes + [weight_pass]:
        copy.wait_send()
    for p in range(4):
        for copy in goes[p] + comes[p]:
            copy.wait_send()
    for j in range(2):
        for h in range(HALVES):
            terms[j][h].wait_send()


def shards(orbitals, occupations):
    vmem = pl.BlockSpec(memory_space=pltpu.VMEM)
    dma = pltpu.SemaphoreType.DMA
    field = (N, SLAB, N)
    return pl.pallas_call(
        kernel,
        out_shape=jax.ShapeDtypeStruct(orbitals.shape, jnp.float32),
        in_specs=[pl.BlockSpec(memory_space=pltpu.SMEM), vmem, vmem],
        out_specs=vmem,
        scratch_shapes=[
            pltpu.VMEM(orbitals.shape, jnp.float32),
            pltpu.VMEM((2, 8, N), jnp.float32),
            pltpu.VMEM((2, 8, N), jnp.float32),
            pltpu.VMEM((4, N, SLAB, N), jnp.float32),
            pltpu.VMEM((4, SLAB, N, N), jnp.float32),
            pltpu.VMEM((4, N, SLAB, N), jnp.float32),
            pltpu.VMEM(orbitals.shape, jnp.float32),
            pltpu.VMEM(orbitals.shape, jnp.float32),
            pltpu.VMEM((SLAB, N, N), jnp.float32),
            pltpu.VMEM((ROWS, N, N), jnp.float32),
            dma((2,)), dma((2,)), dma, dma,
            dma((4, 7)), dma((4, 7)), dma((4, 7)), dma((4, 7)),
            dma((2, HALVES)), dma((2, HALVES)), dma((4, 2)),
        ],
        compiler_params=pltpu.CompilerParams(
            collective_id=0, has_side_effects=True, vmem_limit_bytes=48 * 1024 * 1024
        ),
        name="exchange",
    )(occupations, orbitals, jnp.asarray(tables()))


def solution(mesh):
    placed = (P("band", "pw", None, None), P("band"))
    return jax.shard_map(
        shards, mesh=mesh, in_specs=placed, out_specs=P("band", "pw", None, None), check_vma=False
    )
```

```python
import functools

import jax
import jax.numpy as jnp
import numpy as np
from jax import lax
from jax.experimental import pallas as pl
from jax.experimental.pallas import tpu as pltpu
from jax.sharding import PartitionSpec as P

MIXING = 0.25
N = 128
HALF = N // 2
SLAB = 16
HALVES = 2
ROWS = SLAB // HALVES
MESH = pl.DeviceIdType.MESH
FAR_FIRST = ((2, 1), (2, 0), (1, 1), (3, 1), (0, 1), (1, 0), (3, 0))
PAIRS = ((0, 0), (1, 0), (0, 1), (1, 1))
PARTS = 4
PART = SLAB // PARTS


def tables():
    grid = np.arange(N)
    cosines = [np.cos(2.0 * np.pi * (k * grid % N) / N) for k in range(HALF + 1)]
    sines = [np.sin(2.0 * np.pi * (k * grid % N) / N) for k in range(1, HALF)]
    table = np.stack(cosines + sines, axis=1).astype(np.float32)
    high = table.astype(jnp.bfloat16)
    low = (table - high.astype(np.float32)).astype(jnp.bfloat16)
    right_forward = np.block([[high, low], [high, low]])
    left_forward = np.block([[high.T, high.T], [low.T, low.T]])
    left_inverse = np.block([[high, high], [low, low]])
    right_inverse = np.block([[high.T, low.T], [high.T, low.T]])
    return np.stack([right_forward, left_forward, left_inverse, right_inverse])


def split(value):
    high = value.astype(jnp.bfloat16)
    low = (value - high.astype(jnp.float32)).astype(jnp.bfloat16)
    return high, low


def from_right(value, table):
    high, low = split(value)
    both = jnp.dot(
        jnp.concatenate([high, low], axis=1), table, preferred_element_type=jnp.float32
    )
    return both[:, :N] + both[:, N:]


def from_left(table, value):
    high, low = split(value)
    both = jnp.dot(
        table, jnp.concatenate([high, low], axis=0), preferred_element_type=jnp.float32
    )
    return both[:N] + both[N:]


def side_by_side(value):
    return jnp.concatenate([value[:N], value[N:]], axis=1)


def stacked(value):
    return jnp.concatenate([value[:, :N], value[:, N:]], axis=0)


def wave_numbers(index):
    wave = jnp.where(index > HALF, index - HALF, index)
    share = jnp.where((wave == 0) | (wave == HALF), 1.0 / N, 2.0 / N)
    wave = wave.astype(jnp.float32) * (2.0 * np.pi / N)
    return wave * wave, share


def kernel(
    occupations, orbitals, table, out, passing, weights, passed_weights, sent, middle, back,
    theirs, returned, coulomb, turned, pass_relay, term_relay, pass_send, pass_recv, weight_send,
    weight_recv, go_send, go_recv, come_send, come_recv, term_send, term_recv, local_sem,
    relay_send, relay_recv,
):
    band = lax.axis_index("band")
    place = lax.axis_index("pw")
    bands = lax.axis_size("band")
    ring = bands // 2
    spot, base = lax.rem(band, ring), (band // ring) * ring
    across = lax.rem(base + ring, bands)
    following = {"band": lax.rem(band + 1, bands)}
    previous = {"band": lax.rem(band + bands - 1, bands)}
    place_x, place_y = lax.rem(place, 4), lax.div(place, 4)
    peers = [
        lax.rem(place_y + dy, 2) * 4 + lax.rem(place_x + dx, 4) for dx, dy in FAR_FIRST
    ]
    is_first, is_last = spot == 0, spot == ring - 1
    is_second, is_second_last = spot == 2, spot == ring - 3
    first, last, second, second_last = 0, ring - 1, 2, ring - 3
    pass_relays = (None, last, second, second_last)
    term_relays = (None, first, second_last, second)

    for i in range(2):
        weight = occupations[i].astype(jnp.float32) * (-0.5 * MIXING)
        weights[i] = jnp.full((8, N), weight, jnp.float32)

    barrier = pltpu.get_barrier_semaphore()

    def greet(device):
        pl.semaphore_signal(barrier, inc=1, device_id=device, device_id_type=MESH)

    for device in [following, previous] + [{"pw": peer} for peer in peers]:
        greet(device)
    for here, others in (
        (is_first, ((first, 0), (last, 1), (second, 2), (second_last, 2))),
        (is_last, ((last, 0), (first, 1), (second, 2), (second_last, 2))),
        (is_second, ((first, 2), (last, 2))),
        (is_second_last, ((first, 2), (last, 2))),
    ):

        @pl.when(here)
        def _():
            for other, side in others:
                if side != 0:
                    greet({"band": base + other})
                if side != 1:
                    greet({"band": across + other})

    at_end = (is_first | is_last).astype(jnp.int32)
    beside = (is_second | is_second_last).astype(jnp.int32)
    pl.semaphore_wait(barrier, 2 + len(peers) + 6 * at_end + 4 * beside)

    def part(q):
        return pl.ds(q * PART, PART)

    def routes(source, target, relay, sends, recvs, relay_sends, relay_recvs, onward, relays, end):
        direct, there, then = [], [], []
        for j in range(2):
            for q in range(PARTS):
                direct.append(pltpu.make_async_remote_copy(
                    src_ref=source.at[j, part(q)], dst_ref=target.at[j, part(q)],
                    send_sem=sends.at[j, q], recv_sem=recvs.at[j, q],
                    device_id=onward, device_id_type=MESH,
                ))
                if relays[q] is None:
                    there.append(None)
                    then.append(None)
                    continue
                there.append(pltpu.make_async_remote_copy(
                    src_ref=source.at[j, part(q)], dst_ref=relay.at[j],
                    send_sem=sends.at[j, q], recv_sem=relay_recvs.at[j],
                    device_id={"band": across + relays[q]}, device_id_type=MESH,
                ))
                then.append(pltpu.make_async_remote_copy(
                    src_ref=relay.at[j], dst_ref=target.at[j, part(q)],
                    send_sem=relay_sends.at[j], recv_sem=recvs.at[j, q],
                    device_id={"band": base + end}, device_id_type=MESH,
                ))
        return direct, there, then

    pass_direct, pass_there, pass_then = routes(
        orbitals, passing, pass_relay, pass_send, pass_recv, relay_send.at[0], relay_recv.at[0],
        following, pass_relays, first,
    )
    term_direct, term_there, term_then = routes(
        theirs, returned, term_relay, term_send, term_recv, relay_send.at[1], relay_recv.at[1],
        previous, term_relays, last,
    )

    def start(direct, there, is_end, j, q):
        n = j * PARTS + q
        if there[n] is None:
            direct[n].start()
            return

        @pl.when(is_end)
        def _():
            there[n].start()

        @pl.when(jnp.logical_not(is_end))
        def _():
            direct[n].start()

    roles = {first: is_first, last: is_last, second: is_second, second_last: is_second_last}

    def relay_on(there, then, relays, j):
        for q in range(1, PARTS):
            n = j * PARTS + q

            @pl.when(roles[relays[q]])
            def _():
                there[n].wait_recv()
                then[n].start()

    def relay_end(then, relays):
        for q in range(1, PARTS):

            @pl.when(roles[relays[q]])
            def _():
                for j in range(2):
                    then[j * PARTS + q].wait_send()

    weight_pass = pltpu.make_async_remote_copy(
        src_ref=weights, dst_ref=passed_weights, send_sem=weight_send, recv_sem=weight_recv,
        device_id=following, device_id_type=MESH,
    )
    for j in range(2):
        for q in range(PARTS):
            start(pass_direct, pass_there, is_last, j, q)
    weight_pass.start()

    def slab(index):
        return pl.ds(pl.multiple_of(index * SLAB, SLAB), SLAB)

    goes, comes, stays = [], [], []
    for p in range(4):
        goes.append([
            pltpu.make_async_remote_copy(
                src_ref=sent.at[p, slab(peer)], dst_ref=middle.at[p, :, slab(place)],
                send_sem=go_send.at[p, n], recv_sem=go_recv.at[p, n],
                device_id={"pw": peer}, device_id_type=MESH,
            )
            for n, peer in enumerate(peers)
        ])
        comes.append([
            pltpu.make_async_remote_copy(
                src_ref=middle.at[p, :, slab(peer)], dst_ref=back.at[p, slab(place)],
                send_sem=come_send.at[p, n], recv_sem=come_recv.at[p, n],
                device_id={"pw": peer}, device_id_type=MESH,
            )
            for n, peer in enumerate(peers)
        ])
        stays.append((
            pltpu.make_async_copy(
                sent.at[p, slab(place)], middle.at[p, :, slab(place)], local_sem.at[p, 0]
            ),
            pltpu.make_async_copy(
                middle.at[p, :, slab(place)], back.at[p, slab(place)], local_sem.at[p, 1]
            ),
        ))
    for p, (i, j) in enumerate(PAIRS):
        if i == 0:
            relay_on(pass_there, pass_then, pass_relays, j)
            for q in range(PARTS):
                pass_direct[j * PARTS + q].wait_recv()

        @pl.loop(0, HALVES)
        def _(h):
            @pl.loop(0, ROWS // 4)
            def _(quad):
                for r in range(2):
                    at = pl.ds(h * ROWS + quad * 4 + r * 2, 2)
                    field = (orbitals[i, at] * passing[j, at]).reshape(2 * N, N)
                    field = from_right(field, table[0])
                    field = from_left(table[1], side_by_side(field))
                    turned[quad * 4 + r * 2] = field[:, :N]
                    turned[quad * 4 + r * 2 + 1] = field[:, N:]

            @pl.loop(0, N // 16)
            def _(block):
                for b in range(2):
                    rows = pl.ds(pl.multiple_of(block * 16 + b * 8, 8), 8)
                    sent[p, rows, pl.ds(pl.multiple_of(h * ROWS, ROWS), ROWS)] = jnp.swapaxes(
                        turned[:, rows], 0, 1
                    )

        stays[p][0].start()
        for copy in goes[p]:
            copy.start()
        if p == 1:
            wave_x, share_x = wave_numbers(lax.broadcasted_iota(jnp.int32, (N, N), 0))
            wave_z, share_z = wave_numbers(lax.broadcasted_iota(jnp.int32, (N, N), 1))
            square_xz = wave_x + wave_z
            share_xz = share_x * share_z

            @pl.loop(0, SLAB)
            def _(y):
                wave_y, share_y = wave_numbers(
                    jnp.full((N, N), place * SLAB + y, jnp.int32)
                )
                square = square_xz + wave_y
                safe = jnp.where(square > 0, square, 1.0)
                factor = (4.0 * np.pi) * (share_xz * share_y)
                coulomb[y] = jnp.where(square > 0, factor / safe, 0.0)

    for p in range(4):
        stays[p][0].wait()
        for copy in goes[p]:
            copy.wait_recv()

        @pl.loop(0, SLAB // 4)
        def _(quad):
            for r in range(2):
                y = quad * 4 + r * 2
                field = jnp.concatenate([middle[p, y], middle[p, y + 1]], axis=1)
                field = from_left(table[1], field)
                field = field * jnp.concatenate([coulomb[y], coulomb[y + 1]], axis=1)
                field = from_left(table[2], field)
                middle[p, y] = field[:, :N]
                middle[p, y + 1] = field[:, N:]

        stays[p][1].start()
        for copy in comes[p]:
            copy.start()

    weight_pass.wait_recv()
    for p, (i, j) in enumerate(PAIRS):
        stays[p][1].wait()
        for copy in comes[p]:
            copy.wait_recv()
        for h in range(HALVES):

            @pl.loop(0, N // 16)
            def _(block):
                for b in range(2):
                    rows = pl.ds(pl.multiple_of(block * 16 + b * 8, 8), 8)
                    turned[:, rows] = jnp.swapaxes(back[p, rows, h * ROWS : (h + 1) * ROWS], 0, 1)

            @pl.loop(0, ROWS // 4)
            def _(quad):
                for r in range(2):
                    y = quad * 4 + r * 2
                    field = jnp.concatenate([turned[y], turned[y + 1]], axis=1)
                    field = from_left(table[2], field)
                    field = from_right(stacked(field), table[3])
                    potential = field.reshape(2, N // 8, 8, N)
                    at = pl.ds(h * ROWS + y, 2)
                    mine = (
                        potential * passing[j, at].reshape(2, N // 8, 8, N) * passed_weights[j]
                    ).reshape(2, N, N)
                    other = (
                        potential * orbitals[i, at].reshape(2, N // 8, 8, N) * weights[i]
                    ).reshape(2, N, N)
                    if j == 0:
                        out[i, at] = mine
                    else:
                        out[i, at] += mine
                    if i == 0:
                        theirs[j, at] = other
                    else:
                        theirs[j, at] += other

            if i == 1:
                for q in range(h * PARTS // HALVES, (h + 1) * PARTS // HALVES):
                    start(term_direct, term_there, is_first, j, q)

    for j in range(2):
        relay_on(term_there, term_then, term_relays, j)
    for j in range(2):
        for q in range(PARTS):
            term_direct[j * PARTS + q].wait_recv()

            @pl.loop(0, PART)
            def _(row):
                out[j, q * PART + row] += returned[j, q * PART + row]

    relay_end(pass_then, pass_relays)
    relay_end(term_then, term_relays)
    weight_pass.wait_send()
    for copy in pass_direct + term_direct:
        copy.wait_send()
    for p in range(4):
        for copy in goes[p] + comes[p]:
            copy.wait_send()


def shards(orbitals, occupations):
    vmem = pl.BlockSpec(memory_space=pltpu.VMEM)
    dma = pltpu.SemaphoreType.DMA
    field = (N, SLAB, N)
    return pl.pallas_call(
        kernel,
        out_shape=jax.ShapeDtypeStruct(orbitals.shape, jnp.float32),
        in_specs=[pl.BlockSpec(memory_space=pltpu.SMEM), vmem, vmem],
        out_specs=vmem,
        scratch_shapes=[
            pltpu.VMEM(orbitals.shape, jnp.float32),
            pltpu.VMEM((2, 8, N), jnp.float32),
            pltpu.VMEM((2, 8, N), jnp.float32),
            pltpu.VMEM((4, N, SLAB, N), jnp.float32),
            pltpu.VMEM((4, SLAB, N, N), jnp.float32),
            pltpu.VMEM((4, N, SLAB, N), jnp.float32),
            pltpu.VMEM(orbitals.shape, jnp.float32),
            pltpu.VMEM(orbitals.shape, jnp.float32),
            pltpu.VMEM((SLAB, N, N), jnp.float32),
            pltpu.VMEM((ROWS, N, N), jnp.float32),
            pltpu.VMEM((2, PART, N, N), jnp.float32),
            pltpu.VMEM((2, PART, N, N), jnp.float32),
            dma((2, PARTS)), dma((2, PARTS)), dma, dma,
            dma((4, 7)), dma((4, 7)), dma((4, 7)), dma((4, 7)),
            dma((2, PARTS)), dma((2, PARTS)), dma((4, 2)), dma((2, 2)), dma((2, 2)),
        ],
        compiler_params=pltpu.CompilerParams(
            collective_id=0, has_side_effects=True, vmem_limit_bytes=48 * 1024 * 1024
        ),
        name="exchange",
    )(occupations, orbitals, jnp.asarray(tables()))


def solution(mesh):
    placed = (P("band", "pw", None, None), P("band"))
    return jax.shard_map(
        shards, mesh=mesh, in_specs=placed, out_specs=P("band", "pw", None, None), check_vma=False
    )
```

```python
import functools

import jax
import jax.numpy as jnp
import numpy as np
from jax import lax
from jax.experimental import pallas as pl
from jax.experimental.pallas import tpu as pltpu
from jax.sharding import PartitionSpec as P

MIXING = 0.25
N = 128
HALF = N // 2
SLAB = 16
HALVES = 2
ROWS = SLAB // HALVES
MESH = pl.DeviceIdType.MESH
FAR_FIRST = ((2, 1), (2, 0), (1, 1), (3, 1), (0, 1), (1, 0), (3, 0))
PARTS = 8
TURNS = ((0, 0), (0, 1), (0, 2), (0, 3))
PART = SLAB // PARTS


def tables():
    grid = np.arange(N)
    cosines = [np.cos(2.0 * np.pi * (k * grid % N) / N) for k in range(HALF + 1)]
    sines = [np.sin(2.0 * np.pi * (k * grid % N) / N) for k in range(1, HALF)]
    table = np.stack(cosines + sines, axis=1).astype(np.float32)
    high = table.astype(jnp.bfloat16)
    low = (table - high.astype(np.float32)).astype(jnp.bfloat16)
    right_forward = np.block([[high, low], [high, low]])
    left_forward = np.block([[high.T, high.T], [low.T, low.T]])
    left_inverse = np.block([[high, high], [low, low]])
    right_inverse = np.block([[high.T, low.T], [high.T, low.T]])
    return np.stack([right_forward, left_forward, left_inverse, right_inverse])


def split(value):
    high = value.astype(jnp.bfloat16)
    low = (value - high.astype(jnp.float32)).astype(jnp.bfloat16)
    return high, low


def from_right(value, table):
    high, low = split(value)
    both = jnp.dot(
        jnp.concatenate([high, low], axis=1), table, preferred_element_type=jnp.float32
    )
    return both[:, :N] + both[:, N:]


def from_left(table, value):
    high, low = split(value)
    both = jnp.dot(
        table, jnp.concatenate([high, low], axis=0), preferred_element_type=jnp.float32
    )
    return both[:N] + both[N:]


def side_by_side(value):
    return jnp.concatenate([value[:N], value[N:]], axis=1)


def stacked(value):
    return jnp.concatenate([value[:, :N], value[:, N:]], axis=0)


def wave_numbers(index):
    wave = jnp.where(index > HALF, index - HALF, index)
    share = jnp.where((wave == 0) | (wave == HALF), 1.0 / N, 2.0 / N)
    wave = wave.astype(jnp.float32) * (2.0 * np.pi / N)
    return wave * wave, share


def kernel(
    occupations_in, orbitals_in, table_in, out, occupations, orbitals, table, passing, weights,
    passed_weights, sent, middle, back, theirs, returned, coulomb, turned, pass_relay, term_relay,
    input_sem, pass_send, pass_recv, weight_send, weight_recv, go_send, go_recv, come_send,
    come_recv, term_send, term_recv, relay_send, relay_recv, turn,
):
    inputs = [
        pltpu.make_async_copy(orbitals_in, orbitals, input_sem.at[0]),
        pltpu.make_async_copy(table_in, table, input_sem.at[1]),
        pltpu.make_async_copy(occupations_in, occupations, input_sem.at[2]),
    ]
    for copy in inputs:
        copy.start()
    band = lax.axis_index("band")
    place = lax.axis_index("pw")
    bands = lax.axis_size("band")
    ring = bands // 2
    spot, base = lax.rem(band, ring), (band // ring) * ring
    across = lax.rem(base + ring, bands)
    following = {"band": lax.rem(band + 1, bands)}
    previous = {"band": lax.rem(band + bands - 1, bands)}
    place_x, place_y = lax.rem(place, 4), lax.div(place, 4)
    peers = [
        lax.rem(place_y + dy, 2) * 4 + lax.rem(place_x + dx, 4) for dx, dy in FAR_FIRST
    ]
    first, last = 0, ring - 1
    near_pass, near_term = (None, last) * 4, (None, first + 1) * 4
    far_pass = (3, ring - 3, 5, ring - 5) * 2
    far_term = (ring - 3, ring - 5, ring - 7, ring - 5)
    pass_routes = {(j, q): (near_pass, far_pass)[j][q] for j in range(2) for q in range(PARTS)}
    term_routes = {
        (j, q): (far_term + near_term)[q] for j in range(2) for q in range(PARTS)
    }
    pass_relays = sorted({relay for relay in pass_routes.values() if relay is not None})
    term_relays = sorted({relay for relay in term_routes.values() if relay is not None})

    greetings = {}
    for here, there, far in (
        [(last, relay, True) for relay in pass_relays]
        + [(first, relay, False) for relay in pass_relays]
        + [(first, relay, True) for relay in term_relays]
        + [(last, relay, False) for relay in term_relays]
    ):
        greetings.setdefault(here, []).append((there, far))
        if here != there:
            greetings.setdefault(there, []).append((here, far))

    barrier = pltpu.get_barrier_semaphore()

    def greet(device):
        pl.semaphore_signal(barrier, inc=1, device_id=device, device_id_type=MESH)

    for device in [following, previous] + [{"pw": peer} for peer in peers]:
        greet(device)
    callers = 2 + len(peers)
    for here, others in greetings.items():
        callers = callers + len(others) * (spot == here).astype(jnp.int32)

        @pl.when(spot == here)
        def _():
            for other, far in others:
                greet({"band": (across if far else base) + other})

    pl.semaphore_wait(barrier, callers)

    def part(q):
        return pl.ds(q * PART, PART)

    def routes(source, target, relay, send, recv, relay_sends, relay_recvs, onward, ways, end):
        direct, there, then, taken = {}, {}, {}, {}
        for j in range(2):
            for q in range(PARTS):
                direct[j, q] = pltpu.make_async_remote_copy(
                    src_ref=source.at[j, part(q)], dst_ref=target.at[j, part(q)],
                    send_sem=send.at[j], recv_sem=recv.at[j, q // 4],
                    device_id=onward, device_id_type=MESH,
                )
                spot_of = ways[j, q]
                if spot_of is None:
                    continue
                slot = taken.get(spot_of, 0)
                taken[spot_of] = slot + 1
                there[j, q] = pltpu.make_async_remote_copy(
                    src_ref=source.at[j, part(q)], dst_ref=relay.at[slot],
                    send_sem=send.at[j], recv_sem=relay_recvs.at[slot],
                    device_id={"band": across + spot_of}, device_id_type=MESH,
                )
                then[j, q] = pltpu.make_async_remote_copy(
                    src_ref=relay.at[slot], dst_ref=target.at[j, part(q)],
                    send_sem=relay_sends.at[slot], recv_sem=recv.at[j, q // 4],
                    device_id={"band": base + end}, device_id_type=MESH,
                )
        return direct, there, then

    pass_direct, pass_there, pass_then = routes(
        orbitals_in, passing, pass_relay, pass_send, pass_recv,
        relay_send.at[0], relay_recv.at[0], following, pass_routes, first,
    )
    term_direct, term_there, term_then = routes(
        theirs, returned, term_relay, term_send, term_recv,
        relay_send.at[1], relay_recv.at[1], previous, term_routes, last,
    )

    def start(direct, there, source, parts):
        @pl.when(spot == source)
        def _():
            for where in parts:
                there.get(where, direct[where]).start()

        @pl.when(spot != source)
        def _():
            for where in parts:
                direct[where].start()

    def relay_on(there, then, ways, parts):
        for relay in sorted({ways[where] for where in parts if where in then}):

            @pl.when(spot == relay)
            def _():
                for where in parts:
                    if ways[where] == relay:
                        there[where].wait_recv()
                        then[where].start()

    def relay_end(then, ways):
        for relay in sorted({ways[where] for where in then}):

            @pl.when(spot == relay)
            def _():
                for where, copy in then.items():
                    if ways[where] == relay:
                        copy.wait_send()

    def parts_of(j, h=None):
        return [(j, q) for q in range(PARTS) if h is None or q // 4 == h]

    def arrived(ref, sem):
        pltpu.make_async_copy(ref, ref, sem).wait()

    weight_pass = pltpu.make_async_remote_copy(
        src_ref=weights, dst_ref=passed_weights, send_sem=weight_send, recv_sem=weight_recv,
        device_id=following, device_id_type=MESH,
    )

    start(pass_direct, pass_there, last, parts_of(0))
    relay_on(pass_there, pass_then, pass_routes, parts_of(0))
    start(pass_direct, pass_there, last, parts_of(1))
    for copy in inputs:
        copy.wait()
    for i in range(2):
        weight = occupations[i].astype(jnp.float32) * (-0.5 * MIXING)
        weights[i] = jnp.full((8, N), weight, jnp.float32)
    weight_pass.start()

    def slab(index):
        return pl.ds(pl.multiple_of(index * SLAB, SLAB), SLAB)

    def half(h):
        return pl.ds(h * ROWS, ROWS)

    def half_of(index, h):
        return pl.ds(pl.multiple_of(index * SLAB + h * ROWS, ROWS), ROWS)

    def go(p, h):
        pltpu.make_async_copy(
            sent.at[p, slab(place), half(h)], middle.at[p, :, half_of(place, h)], go_recv.at[p]
        ).start()
        for peer in peers:
            pltpu.make_async_remote_copy(
                src_ref=sent.at[p, slab(peer), half(h)],
                dst_ref=middle.at[p, :, half_of(place, h)],
                send_sem=go_send.at[p], recv_sem=go_recv.at[p],
                device_id={"pw": peer}, device_id_type=MESH,
            ).start()

    def come(p, h):
        pltpu.make_async_copy(
            middle.at[p, :, half_of(place, h)], back.at[p, slab(place), half(h)],
            come_recv.at[p, h],
        ).start()
        for peer in peers:
            pltpu.make_async_remote_copy(
                src_ref=middle.at[p, :, half_of(peer, h)],
                dst_ref=back.at[p, slab(place), half(h)],
                send_sem=come_send.at[p], recv_sem=come_recv.at[p, h],
                device_id={"pw": peer}, device_id_type=MESH,
            ).start()

    def forward(i, j, p, h):
        @pl.loop(0, ROWS // 4)
        def _(quad):
            for r in range(2):
                at = pl.ds(h * ROWS + quad * 4 + r * 2, 2)
                field = (orbitals[i, at] * passing[j, at]).reshape(2 * N, N)
                field = from_right(field, table[0])
                field = from_left(table[1], side_by_side(field))
                turned[quad * 4 + r * 2] = field[:, :N]
                turned[quad * 4 + r * 2 + 1] = field[:, N:]

        @pl.loop(0, N // 16)
        def _(block):
            for b in range(2):
                rows = pl.ds(pl.multiple_of(block * 16 + b * 8, 8), 8)
                sent[p, rows, half(h)] = jnp.swapaxes(turned[:, rows], 0, 1)

    for j in range(2):
        for h in range(HALVES):
            arrived(passing.at[j, half(h)], pass_recv.at[j, h])
            for i in range(2):
                forward(i, j, 2 * j + i, h)
                go(2 * j + i, h)
        if j == 0:
            wave_x, share_x = wave_numbers(lax.broadcasted_iota(jnp.int32, (N, N), 0))
            wave_z, share_z = wave_numbers(lax.broadcasted_iota(jnp.int32, (N, N), 1))
            square_xz = wave_x + wave_z
            share_xz = share_x * share_z

            @pl.loop(0, SLAB)
            def _(y):
                wave_y, share_y = wave_numbers(
                    jnp.full((N, N), place * SLAB + y, jnp.int32)
                )
                square = square_xz + wave_y
                safe = jnp.where(square > 0, square, 1.0)
                factor = (4.0 * np.pi) * (share_xz * share_y)
                coulomb[y] = jnp.where(square > 0, factor / safe, 0.0)

    relay_on(pass_there, pass_then, pass_routes, parts_of(1))

    for p in range(4):
        arrived(middle.at[p], go_recv.at[p])

        @pl.loop(0, SLAB // 4)
        def _(quad):
            for r in range(2):
                y = quad * 4 + r * 2
                field = jnp.concatenate([middle[p, y], middle[p, y + 1]], axis=1)
                field = from_left(table[1], field)
                field = field * jnp.concatenate([coulomb[y], coulomb[y + 1]], axis=1)
                field = from_left(table[2], field)
                middle[p, y] = field[:, :N]
                middle[p, y + 1] = field[:, N:]

        come(p, 0)
    core = lax.rem(band, 2)

    @pl.when(core == 0)
    def _():
        for p in range(4):
            come(p, 1)

    for p in range(4):
        if TURNS[p] is None:
            pl.when(core == 1)(functools.partial(come, p, 1))

    weight_pass.wait_recv()
    for h in range(HALVES):
        for j in range(2):
            for i in range(2):
                p = 2 * j + i
                if (h, p) == (1, 2):
                    relay_on(term_there, term_then, term_routes, parts_of(0, 0) + parts_of(1, 0))
                for late in range(4):
                    if TURNS[late] == (h, p):

                        @pl.when(core == 1)
                        def _():
                            pl.semaphore_wait(turn, 1)
                            come(late, 1)

                arrived(back.at[p, :, half(h)], come_recv.at[p, h])
                for late in range(4):
                    if TURNS[late] == (h, p):

                        @pl.when(core == 0)
                        def _():
                            pl.semaphore_signal(
                                turn, inc=1, device_id=following, device_id_type=MESH
                            )


                @pl.loop(0, N // 16)
                def _(block):
                    for b in range(2):
                        rows = pl.ds(pl.multiple_of(block * 16 + b * 8, 8), 8)
                        turned[:, rows] = jnp.swapaxes(back[p, rows, half(h)], 0, 1)

                def backward(quad):
                    for r in range(2):
                        y = quad * 4 + r * 2
                        field = jnp.concatenate([turned[y], turned[y + 1]], axis=1)
                        field = from_left(table[2], field)
                        field = from_right(stacked(field), table[3])
                        potential = field.reshape(2, N // 8, 8, N)
                        at = pl.ds(h * ROWS + y, 2)
                        mine = (
                            potential * passing[j, at].reshape(2, N // 8, 8, N) * passed_weights[j]
                        ).reshape(2, N, N)
                        other = (
                            potential * orbitals[i, at].reshape(2, N // 8, 8, N) * weights[i]
                        ).reshape(2, N, N)
                        if j == 0:
                            out[i, at] = mine
                        else:
                            out[i, at] += mine
                        if i == 0:
                            theirs[j, at] = other
                        else:
                            theirs[j, at] += other

                if i == 0:
                    pl.loop(0, ROWS // 4)(backward)
                else:
                    for quad in range(ROWS // 4):
                        backward(quad)
                        q = 4 * h + 2 * quad
                        start(term_direct, term_there, first, [(j, q), (j, q + 1)])

    relay_on(term_there, term_then, term_routes, parts_of(0, 1) + parts_of(1, 1))
    for h in range(HALVES):
        for j in range(2):
            arrived(returned.at[j, half(h)], term_recv.at[j, h])

            @pl.loop(0, ROWS)
            def _(row):
                out[j, h * ROWS + row] += returned[j, h * ROWS + row]

    relay_end(pass_then, pass_routes)
    relay_end(term_then, term_routes)
    weight_pass.wait_send()
    for j in range(2):
        arrived(passing.at[j], pass_send.at[j])
        arrived(theirs.at[j], term_send.at[j])
    for p in range(4):
        others = pl.ds(0, N - SLAB)
        arrived(sent.at[p, others], go_send.at[p])
        arrived(back.at[p, others], come_send.at[p])


def shards(orbitals, occupations):
    vmem = pl.BlockSpec(memory_space=pltpu.VMEM)
    dma = pltpu.SemaphoreType.DMA
    hbm = pl.BlockSpec(memory_space=pltpu.HBM)
    return pl.pallas_call(
        kernel,
        out_shape=jax.ShapeDtypeStruct(orbitals.shape, jnp.float32),
        in_specs=[hbm, hbm, hbm],
        out_specs=vmem,
        scratch_shapes=[
            pltpu.SMEM(occupations.shape, jnp.int32),
            pltpu.VMEM(orbitals.shape, jnp.float32),
            pltpu.VMEM((4, 2 * N, 2 * N), jnp.bfloat16),
            pltpu.VMEM(orbitals.shape, jnp.float32),
            pltpu.VMEM((2, 8, N), jnp.float32),
            pltpu.VMEM((2, 8, N), jnp.float32),
            pltpu.VMEM((4, N, SLAB, N), jnp.float32),
            pltpu.VMEM((4, SLAB, N, N), jnp.float32),
            pltpu.VMEM((4, N, SLAB, N), jnp.float32),
            pltpu.VMEM(orbitals.shape, jnp.float32),
            pltpu.VMEM(orbitals.shape, jnp.float32),
            pltpu.VMEM((SLAB, N, N), jnp.float32),
            pltpu.VMEM((ROWS, N, N), jnp.float32),
            pltpu.VMEM((PARTS, PART, N, N), jnp.float32),
            pltpu.VMEM((PARTS, PART, N, N), jnp.float32),
            dma((3,)), dma((2,)), dma((2, HALVES)), dma, dma, dma((4,)), dma((4,)), dma((4,)),
            dma((4, HALVES)), dma((2,)), dma((2, HALVES)), dma((2, PARTS)), dma((2, PARTS)),
            pltpu.SemaphoreType.REGULAR,
        ],
        compiler_params=pltpu.CompilerParams(
            collective_id=0, has_side_effects=True, vmem_limit_bytes=48 * 1024 * 1024
        ),
        name="exchange",
    )(*(
        pltpu.with_memory_space_constraint(operand, pltpu.HBM)
        for operand in (occupations, orbitals, jnp.asarray(tables()))
    ))


def solution(mesh):
    placed = (P("band", "pw", None, None), P("band"))
    return jax.shard_map(
        shards, mesh=mesh, in_specs=placed, out_specs=P("band", "pw", None, None), check_vma=False
    )
```

```python
import functools

import jax
import jax.numpy as jnp
import numpy as np
from jax import lax
from jax.experimental import pallas as pl
from jax.experimental.pallas import tpu as pltpu
from jax.sharding import PartitionSpec as P

MIXING = 0.25
N = 128
HALF = N // 2
SLAB = 16
HALVES = 2
ROWS = SLAB // HALVES
MESH = pl.DeviceIdType.MESH
FAR_FIRST = ((2, 1), (2, 0), (1, 1), (3, 1), (0, 1), (1, 0), (3, 0))
PARTS = 8
FIRST_TURNS = (None, None, None, 2)
TURNS = ((0, 3), (1, 0), (1, 1), (1, 2))
PART = SLAB // PARTS


def tables():
    grid = np.arange(N)
    cosines = [np.cos(2.0 * np.pi * (k * grid % N) / N) for k in range(HALF + 1)]
    sines = [np.sin(2.0 * np.pi * (k * grid % N) / N) for k in range(1, HALF)]
    table = np.stack(cosines + sines, axis=1).astype(np.float32)
    high = table.astype(jnp.bfloat16)
    low = (table - high.astype(np.float32)).astype(jnp.bfloat16)
    right_forward = np.block([[high, low], [high, low]])
    left_forward = np.block([[high.T, high.T], [low.T, low.T]])
    left_inverse = np.block([[high, high], [low, low]])
    right_inverse = np.block([[high.T, low.T], [high.T, low.T]])
    return np.stack([right_forward, left_forward, left_inverse, right_inverse])


def split(value):
    high = value.astype(jnp.bfloat16)
    low = (value - high.astype(jnp.float32)).astype(jnp.bfloat16)
    return high, low


def from_right(value, table):
    high, low = split(value)
    both = jnp.dot(
        jnp.concatenate([high, low], axis=1), table, preferred_element_type=jnp.float32
    )
    return both[:, :N] + both[:, N:]


def from_left(table, value):
    high, low = split(value)
    both = jnp.dot(
        table, jnp.concatenate([high, low], axis=0), preferred_element_type=jnp.float32
    )
    return both[:N] + both[N:]


def side_by_side(value):
    return jnp.concatenate([value[:N], value[N:]], axis=1)


def stacked(value):
    return jnp.concatenate([value[:, :N], value[:, N:]], axis=0)


def wave_numbers(index):
    wave = jnp.where(index > HALF, index - HALF, index)
    share = jnp.where((wave == 0) | (wave == HALF), 1.0 / N, 2.0 / N)
    wave = wave.astype(jnp.float32) * (2.0 * np.pi / N)
    return wave * wave, share


def kernel(
    occupations_in, orbitals_in, table_in, out, occupations, orbitals, table, passing, weights,
    passed_weights, sent, middle, back, theirs, returned, coulomb, turned, pass_relay, term_relay,
    input_sem, pass_send, pass_recv, weight_send, weight_recv, go_send, go_recv, come_send,
    come_recv, term_send, term_recv, relay_send, relay_recv, turn,
):
    inputs = [
        pltpu.make_async_copy(orbitals_in, orbitals, input_sem.at[0]),
        pltpu.make_async_copy(table_in, table, input_sem.at[1]),
        pltpu.make_async_copy(occupations_in, occupations, input_sem.at[2]),
    ]
    for copy in inputs:
        copy.start()
    band = lax.axis_index("band")
    place = lax.axis_index("pw")
    bands = lax.axis_size("band")
    ring = bands // 2
    spot, base = lax.rem(band, ring), (band // ring) * ring
    across = lax.rem(base + ring, bands)
    following = {"band": lax.rem(band + 1, bands)}
    previous = {"band": lax.rem(band + bands - 1, bands)}
    place_x, place_y = lax.rem(place, 4), lax.div(place, 4)
    peers = [
        lax.rem(place_y + dy, 2) * 4 + lax.rem(place_x + dx, 4) for dx, dy in FAR_FIRST
    ]
    first, last = 0, ring - 1
    near_pass, near_term = (None, last, None, last, None, last, 7, 7), (None, first + 1) * 4
    far_pass = (3, 3, 5, 7, 3, ring - 3, 5, 7)
    far_term = (ring - 3, ring - 5, ring - 7, ring - 5)
    late_term = ((None, first + 1, first + 1, ring - 7), (None, first + 1, None, first + 1))
    pass_routes = {(j, q): (near_pass, far_pass)[j][q] for j in range(2) for q in range(PARTS)}
    term_routes = {
        (j, q): (far_term + late_term[j])[q] for j in range(2) for q in range(PARTS)
    }
    pass_relays = sorted({relay for relay in pass_routes.values() if relay is not None})
    term_relays = sorted({relay for relay in term_routes.values() if relay is not None})

    greetings = {}
    for here, there, far in (
        [(last, relay, True) for relay in pass_relays]
        + [(first, relay, False) for relay in pass_relays]
        + [(first, relay, True) for relay in term_relays]
        + [(last, relay, False) for relay in term_relays]
    ):
        greetings.setdefault(here, []).append((there, far))
        if here != there:
            greetings.setdefault(there, []).append((here, far))

    barrier = pltpu.get_barrier_semaphore()

    def greet(device):
        pl.semaphore_signal(barrier, inc=1, device_id=device, device_id_type=MESH)

    for device in [following, previous] + [{"pw": peer} for peer in peers]:
        greet(device)
    callers = 2 + len(peers)
    for here, others in greetings.items():
        callers = callers + len(others) * (spot == here).astype(jnp.int32)

        @pl.when(spot == here)
        def _():
            for other, far in others:
                greet({"band": (across if far else base) + other})

    pl.semaphore_wait(barrier, callers)

    def part(q):
        return pl.ds(q * PART, PART)

    def routes(source, target, relay, send, recv, relay_sends, relay_recvs, onward, ways, end):
        direct, there, then, taken = {}, {}, {}, {}
        for j in range(2):
            for q in range(PARTS):
                direct[j, q] = pltpu.make_async_remote_copy(
                    src_ref=source.at[j, part(q)], dst_ref=target.at[j, part(q)],
                    send_sem=send.at[j], recv_sem=recv.at[j, q // 4],
                    device_id=onward, device_id_type=MESH,
                )
                spot_of = ways[j, q]
                if spot_of is None:
                    continue
                slot = taken.get(spot_of, 0)
                taken[spot_of] = slot + 1
                there[j, q] = pltpu.make_async_remote_copy(
                    src_ref=source.at[j, part(q)], dst_ref=relay.at[slot],
                    send_sem=send.at[j], recv_sem=relay_recvs.at[slot],
                    device_id={"band": across + spot_of}, device_id_type=MESH,
                )
                then[j, q] = pltpu.make_async_remote_copy(
                    src_ref=relay.at[slot], dst_ref=target.at[j, part(q)],
                    send_sem=relay_sends.at[slot], recv_sem=recv.at[j, q // 4],
                    device_id={"band": base + end}, device_id_type=MESH,
                )
        return direct, there, then

    pass_direct, pass_there, pass_then = routes(
        orbitals_in, passing, pass_relay, pass_send, pass_recv,
        relay_send.at[0], relay_recv.at[0], following, pass_routes, first,
    )
    term_direct, term_there, term_then = routes(
        theirs, returned, term_relay, term_send, term_recv,
        relay_send.at[1], relay_recv.at[1], previous, term_routes, last,
    )

    def start(direct, there, source, parts):
        @pl.when(spot == source)
        def _():
            for where in parts:
                there.get(where, direct[where]).start()

        @pl.when(spot != source)
        def _():
            for where in parts:
                direct[where].start()

    def relay_on(there, then, ways, parts):
        for relay in sorted({ways[where] for where in parts if where in then}):

            @pl.when(spot == relay)
            def _():
                for where in parts:
                    if ways[where] == relay:
                        there[where].wait_recv()
                        then[where].start()

    def relay_end(then, ways):
        for relay in sorted({ways[where] for where in then}):

            @pl.when(spot == relay)
            def _():
                for where, copy in then.items():
                    if ways[where] == relay:
                        copy.wait_send()

    def parts_of(j, h=None):
        return [(j, q) for q in range(PARTS) if h is None or q // 4 == h]

    def arrived(ref, sem):
        pltpu.make_async_copy(ref, ref, sem).wait()

    weight_pass = pltpu.make_async_remote_copy(
        src_ref=weights, dst_ref=passed_weights, send_sem=weight_send, recv_sem=weight_recv,
        device_id=following, device_id_type=MESH,
    )

    start(pass_direct, pass_there, last, parts_of(0))
    prompt = [where for where in parts_of(0) if pass_routes[where] == last]
    relay_on(pass_there, pass_then, pass_routes, prompt)
    start(pass_direct, pass_there, last, parts_of(1))
    for copy in inputs:
        copy.wait()
    for i in range(2):
        weight = occupations[i].astype(jnp.float32) * (-0.5 * MIXING)
        weights[i] = jnp.full((8, N), weight, jnp.float32)
    weight_pass.start()

    def slab(index):
        return pl.ds(pl.multiple_of(index * SLAB, SLAB), SLAB)

    def half(h):
        return pl.ds(h * ROWS, ROWS)

    def half_of(index, h):
        return pl.ds(pl.multiple_of(index * SLAB + h * ROWS, ROWS), ROWS)

    def go(p, h):
        pltpu.make_async_copy(
            sent.at[p, slab(place), half(h)], middle.at[p, :, half_of(place, h)], go_recv.at[p]
        ).start()
        for peer in peers:
            pltpu.make_async_remote_copy(
                src_ref=sent.at[p, slab(peer), half(h)],
                dst_ref=middle.at[p, :, half_of(place, h)],
                send_sem=go_send.at[p], recv_sem=go_recv.at[p],
                device_id={"pw": peer}, device_id_type=MESH,
            ).start()

    def come(p, h):
        pltpu.make_async_copy(
            middle.at[p, :, half_of(place, h)], back.at[p, slab(place), half(h)],
            come_recv.at[p, h],
        ).start()
        for peer in peers:
            pltpu.make_async_remote_copy(
                src_ref=middle.at[p, :, half_of(peer, h)],
                dst_ref=back.at[p, slab(place), half(h)],
                send_sem=come_send.at[p], recv_sem=come_recv.at[p, h],
                device_id={"pw": peer}, device_id_type=MESH,
            ).start()

    def forward(i, j, p, h):
        @pl.loop(0, ROWS // 4)
        def _(quad):
            for r in range(2):
                at = pl.ds(h * ROWS + quad * 4 + r * 2, 2)
                field = (orbitals[i, at] * passing[j, at]).reshape(2 * N, N)
                field = from_right(field, table[0])
                field = from_left(table[1], side_by_side(field))
                turned[quad * 4 + r * 2] = field[:, :N]
                turned[quad * 4 + r * 2 + 1] = field[:, N:]

        @pl.loop(0, N // 16)
        def _(block):
            for b in range(2):
                rows = pl.ds(pl.multiple_of(block * 16 + b * 8, 8), 8)
                sent[p, rows, half(h)] = jnp.swapaxes(turned[:, rows], 0, 1)

    for j in range(2):
        for h in range(HALVES):
            arrived(passing.at[j, half(h)], pass_recv.at[j, h])
            for i in range(2):
                forward(i, j, 2 * j + i, h)
                go(2 * j + i, h)
        if j == 0:
            wave_x, share_x = wave_numbers(lax.broadcasted_iota(jnp.int32, (N, N), 0))
            wave_z, share_z = wave_numbers(lax.broadcasted_iota(jnp.int32, (N, N), 1))
            square_xz = wave_x + wave_z
            share_xz = share_x * share_z

            @pl.loop(0, SLAB)
            def _(y):
                wave_y, share_y = wave_numbers(
                    jnp.full((N, N), place * SLAB + y, jnp.int32)
                )
                square = square_xz + wave_y
                safe = jnp.where(square > 0, square, 1.0)
                factor = (4.0 * np.pi) * (share_xz * share_y)
                coulomb[y] = jnp.where(square > 0, factor / safe, 0.0)

    relay_on(
        pass_there, pass_then, pass_routes,
        [where for j in range(2) for where in parts_of(j) if where not in prompt],
    )

    core = lax.rem(band, 2)
    for p in range(4):
        arrived(middle.at[p], go_recv.at[p])
        signals = FIRST_TURNS.count(p)
        if signals:

            @pl.when(core == 0)
            def _():
                pl.semaphore_signal(turn, inc=signals, device_id=following, device_id_type=MESH)


        @pl.loop(0, SLAB // 4)
        def _(quad):
            for r in range(2):
                y = quad * 4 + r * 2
                field = jnp.concatenate([middle[p, y], middle[p, y + 1]], axis=1)
                field = from_left(table[1], field)
                field = field * jnp.concatenate([coulomb[y], coulomb[y + 1]], axis=1)
                field = from_left(table[2], field)
                middle[p, y] = field[:, :N]
                middle[p, y + 1] = field[:, N:]

        if FIRST_TURNS[p] is not None:

            @pl.when(core == 1)
            def _():
                pl.semaphore_wait(turn, 1)

        come(p, 0)


    @pl.when(core == 0)
    def _():
        for p in range(4):
            come(p, 1)

    for p in range(4):
        if TURNS[p] is None:
            pl.when(core == 1)(functools.partial(come, p, 1))

    weight_pass.wait_recv()
    for h in range(HALVES):
        for j in range(2):
            for i in range(2):
                p = 2 * j + i
                if (h, p) == (1, 2):
                    relay_on(term_there, term_then, term_routes, parts_of(0, 0) + parts_of(1, 0))
                for late in range(4):
                    if TURNS[late] == (h, p):

                        @pl.when(core == 1)
                        def _():
                            pl.semaphore_wait(turn, 1)
                            come(late, 1)

                arrived(back.at[p, :, half(h)], come_recv.at[p, h])
                for late in range(4):
                    if TURNS[late] == (h, p):

                        @pl.when(core == 0)
                        def _():
                            pl.semaphore_signal(
                                turn, inc=1, device_id=following, device_id_type=MESH
                            )


                @pl.loop(0, N // 16)
                def _(block):
                    for b in range(2):
                        rows = pl.ds(pl.multiple_of(block * 16 + b * 8, 8), 8)
                        turned[:, rows] = jnp.swapaxes(back[p, rows, half(h)], 0, 1)

                def backward(quad):
                    for r in range(2):
                        y = quad * 4 + r * 2
                        field = jnp.concatenate([turned[y], turned[y + 1]], axis=1)
                        field = from_left(table[2], field)
                        field = from_right(stacked(field), table[3])
                        potential = field.reshape(2, N // 8, 8, N)
                        at = pl.ds(h * ROWS + y, 2)
                        mine = (
                            potential * passing[j, at].reshape(2, N // 8, 8, N) * passed_weights[j]
                        ).reshape(2, N, N)
                        other = (
                            potential * orbitals[i, at].reshape(2, N // 8, 8, N) * weights[i]
                        ).reshape(2, N, N)
                        if j == 0:
                            out[i, at] = mine
                        else:
                            out[i, at] += mine
                        if i == 0:
                            theirs[j, at] = other
                        else:
                            theirs[j, at] += other

                if i == 0:
                    pl.loop(0, ROWS // 4)(backward)
                else:
                    for quad in range(ROWS // 4):
                        backward(quad)
                        q = 4 * h + 2 * quad
                        start(term_direct, term_there, first, [(j, q), (j, q + 1)])

    relay_on(term_there, term_then, term_routes, parts_of(0, 1) + parts_of(1, 1))
    for h in range(HALVES):
        for j in range(2):
            arrived(returned.at[j, half(h)], term_recv.at[j, h])

            @pl.loop(0, ROWS)
            def _(row):
                out[j, h * ROWS + row] += returned[j, h * ROWS + row]

    relay_end(pass_then, pass_routes)
    relay_end(term_then, term_routes)
    weight_pass.wait_send()
    for j in range(2):
        arrived(passing.at[j], pass_send.at[j])
        arrived(theirs.at[j], term_send.at[j])
    for p in range(4):
        others = pl.ds(0, N - SLAB)
        arrived(sent.at[p, others], go_send.at[p])
        arrived(back.at[p, others], come_send.at[p])


def shards(orbitals, occupations):
    vmem = pl.BlockSpec(memory_space=pltpu.VMEM)
    dma = pltpu.SemaphoreType.DMA
    hbm = pl.BlockSpec(memory_space=pltpu.HBM)
    return pl.pallas_call(
        kernel,
        out_shape=jax.ShapeDtypeStruct(orbitals.shape, jnp.float32),
        in_specs=[hbm, hbm, hbm],
        out_specs=vmem,
        scratch_shapes=[
            pltpu.SMEM(occupations.shape, jnp.int32),
            pltpu.VMEM(orbitals.shape, jnp.float32),
            pltpu.VMEM((4, 2 * N, 2 * N), jnp.bfloat16),
            pltpu.VMEM(orbitals.shape, jnp.float32),
            pltpu.VMEM((2, 8, N), jnp.float32),
            pltpu.VMEM((2, 8, N), jnp.float32),
            pltpu.VMEM((4, N, SLAB, N), jnp.float32),
            pltpu.VMEM((4, SLAB, N, N), jnp.float32),
            pltpu.VMEM((4, N, SLAB, N), jnp.float32),
            pltpu.VMEM(orbitals.shape, jnp.float32),
            pltpu.VMEM(orbitals.shape, jnp.float32),
            pltpu.VMEM((SLAB, N, N), jnp.float32),
            pltpu.VMEM((ROWS, N, N), jnp.float32),
            pltpu.VMEM((PARTS, PART, N, N), jnp.float32),
            pltpu.VMEM((PARTS, PART, N, N), jnp.float32),
            dma((3,)), dma((2,)), dma((2, HALVES)), dma, dma, dma((4,)), dma((4,)), dma((4,)),
            dma((4, HALVES)), dma((2,)), dma((2, HALVES)), dma((2, PARTS)), dma((2, PARTS)),
            pltpu.SemaphoreType.REGULAR,
        ],
        compiler_params=pltpu.CompilerParams(
            collective_id=0, has_side_effects=True, vmem_limit_bytes=48 * 1024 * 1024
        ),
        name="exchange",
    )(*(
        pltpu.with_memory_space_constraint(operand, pltpu.HBM)
        for operand in (occupations, orbitals, jnp.asarray(tables()))
    ))


def solution(mesh):
    placed = (P("band", "pw", None, None), P("band"))
    return jax.shard_map(
        shards, mesh=mesh, in_specs=placed, out_specs=P("band", "pw", None, None), check_vma=False
    )
```

```python
import functools

import jax
import jax.numpy as jnp
import numpy as np
from jax import lax
from jax.experimental import pallas as pl
from jax.experimental.pallas import tpu as pltpu
from jax.sharding import PartitionSpec as P

MIXING = 0.25
N = 128
HALF = N // 2
SLAB = 16
HALVES = 2
ROWS = SLAB // HALVES
MESH = pl.DeviceIdType.MESH
FAR_FIRST = ((2, 1), (1, 0), (3, 0), (0, 1), (2, 0), (1, 1), (3, 1))
PARTS = 8
FIRST_TURNS = (None, None, None, 2)
TURNS = ((0, 3), (1, 0), (1, 1), (1, 2))
PART = SLAB // PARTS


def tables():
    grid = np.arange(N)
    cosines = [np.cos(2.0 * np.pi * (k * grid % N) / N) for k in range(HALF + 1)]
    sines = [np.sin(2.0 * np.pi * (k * grid % N) / N) for k in range(1, HALF)]
    table = np.stack(cosines + sines, axis=1).astype(np.float32)
    high = table.astype(jnp.bfloat16)
    low = (table - high.astype(np.float32)).astype(jnp.bfloat16)
    right_forward = np.block([[high, low], [high, low]])
    left_forward = np.block([[high.T, high.T], [low.T, low.T]])
    left_inverse = np.block([[high, high], [low, low]])
    right_inverse = np.block([[high.T, low.T], [high.T, low.T]])
    return np.stack([right_forward, left_forward, left_inverse, right_inverse])


def split(value):
    high = value.astype(jnp.bfloat16)
    low = (value - high.astype(jnp.float32)).astype(jnp.bfloat16)
    return high, low


def from_right(value, table):
    high, low = split(value)
    both = jnp.dot(
        jnp.concatenate([high, low], axis=1), table, preferred_element_type=jnp.float32
    )
    return both[:, :N] + both[:, N:]


def from_left(table, value):
    high, low = split(value)
    both = jnp.dot(
        table, jnp.concatenate([high, low], axis=0), preferred_element_type=jnp.float32
    )
    return both[:N] + both[N:]


def side_by_side(value):
    return jnp.concatenate([value[:N], value[N:]], axis=1)


def stacked(value):
    return jnp.concatenate([value[:, :N], value[:, N:]], axis=0)


def wave_numbers(index):
    wave = jnp.where(index > HALF, index - HALF, index)
    share = jnp.where((wave == 0) | (wave == HALF), 1.0 / N, 2.0 / N)
    wave = wave.astype(jnp.float32) * (2.0 * np.pi / N)
    return wave * wave, share


def kernel(
    occupations_in, orbitals_in, table_in, out, occupations, orbitals, table, passing, weights,
    passed_weights, sent, middle, back, theirs, returned, coulomb, turned, pass_relay, term_relay,
    input_sem, pass_send, pass_recv, weight_send, weight_recv, go_send, go_recv, come_send,
    come_recv, term_send, term_recv, relay_send, relay_recv, turn,
):
    inputs = [
        pltpu.make_async_copy(orbitals_in, orbitals, input_sem.at[0]),
        pltpu.make_async_copy(table_in, table, input_sem.at[1]),
        pltpu.make_async_copy(occupations_in, occupations, input_sem.at[2]),
    ]
    for copy in inputs:
        copy.start()
    band = lax.axis_index("band")
    place = lax.axis_index("pw")
    bands = lax.axis_size("band")
    ring = bands // 2
    spot, base = lax.rem(band, ring), (band // ring) * ring
    across = lax.rem(base + ring, bands)
    following = {"band": lax.rem(band + 1, bands)}
    previous = {"band": lax.rem(band + bands - 1, bands)}
    place_x, place_y = lax.rem(place, 4), lax.div(place, 4)
    peers = [
        lax.rem(place_y + dy, 2) * 4 + lax.rem(place_x + dx, 4) for dx, dy in FAR_FIRST
    ]
    first, last = 0, ring - 1
    near_pass, near_term = (None, last, None, last, None, last, 7, 7), (None, first + 1) * 4
    far_pass = (3, 3, 5, 7, 3, ring - 3, 5, 7)
    far_term = (ring - 3, ring - 5, ring - 7, ring - 5)
    late_term = ((None, first + 1, first + 1, ring - 7), (None, first + 1, None, first + 1))
    pass_routes = {(j, q): (near_pass, far_pass)[j][q] for j in range(2) for q in range(PARTS)}
    term_routes = {
        (j, q): (far_term + late_term[j])[q] for j in range(2) for q in range(PARTS)
    }
    pass_relays = sorted({relay for relay in pass_routes.values() if relay is not None})
    term_relays = sorted({relay for relay in term_routes.values() if relay is not None})

    greetings = {}
    for here, there, far in (
        [(last, relay, True) for relay in pass_relays]
        + [(first, relay, False) for relay in pass_relays]
        + [(first, relay, True) for relay in term_relays]
        + [(last, relay, False) for relay in term_relays]
    ):
        greetings.setdefault(here, []).append((there, far))
        if here != there:
            greetings.setdefault(there, []).append((here, far))

    barrier = pltpu.get_barrier_semaphore()

    def greet(device):
        pl.semaphore_signal(barrier, inc=1, device_id=device, device_id_type=MESH)

    for device in [following, previous] + [{"pw": peer} for peer in peers]:
        greet(device)
    callers = 2 + len(peers)
    for here, others in greetings.items():
        callers = callers + len(others) * (spot == here).astype(jnp.int32)

        @pl.when(spot == here)
        def _():
            for other, far in others:
                greet({"band": (across if far else base) + other})

    pl.semaphore_wait(barrier, callers)

    def part(q):
        return pl.ds(q * PART, PART)

    def routes(source, target, relay, send, recv, relay_sends, relay_recvs, onward, ways, end):
        direct, there, then, taken = {}, {}, {}, {}
        for j in range(2):
            for q in range(PARTS):
                direct[j, q] = pltpu.make_async_remote_copy(
                    src_ref=source.at[j, part(q)], dst_ref=target.at[j, part(q)],
                    send_sem=send.at[j], recv_sem=recv.at[j, q // 4],
                    device_id=onward, device_id_type=MESH,
                )
                spot_of = ways[j, q]
                if spot_of is None:
                    continue
                slot = taken.get(spot_of, 0)
                taken[spot_of] = slot + 1
                there[j, q] = pltpu.make_async_remote_copy(
                    src_ref=source.at[j, part(q)], dst_ref=relay.at[slot],
                    send_sem=send.at[j], recv_sem=relay_recvs.at[slot],
                    device_id={"band": across + spot_of}, device_id_type=MESH,
                )
                then[j, q] = pltpu.make_async_remote_copy(
                    src_ref=relay.at[slot], dst_ref=target.at[j, part(q)],
                    send_sem=relay_sends.at[slot], recv_sem=recv.at[j, q // 4],
                    device_id={"band": base + end}, device_id_type=MESH,
                )
        return direct, there, then

    pass_direct, pass_there, pass_then = routes(
        orbitals_in, passing, pass_relay, pass_send, pass_recv,
        relay_send.at[0], relay_recv.at[0], following, pass_routes, first,
    )
    term_direct, term_there, term_then = routes(
        theirs, returned, term_relay, term_send, term_recv,
        relay_send.at[1], relay_recv.at[1], previous, term_routes, last,
    )

    def start(direct, there, source, parts):
        @pl.when(spot == source)
        def _():
            for where in parts:
                there.get(where, direct[where]).start()

        @pl.when(spot != source)
        def _():
            for where in parts:
                direct[where].start()

    def relay_on(there, then, ways, parts):
        for relay in sorted({ways[where] for where in parts if where in then}):

            @pl.when(spot == relay)
            def _():
                for where in parts:
                    if ways[where] == relay:
                        there[where].wait_recv()
                        then[where].start()

    def relay_end(then, ways):
        for relay in sorted({ways[where] for where in then}):

            @pl.when(spot == relay)
            def _():
                for where, copy in then.items():
                    if ways[where] == relay:
                        copy.wait_send()

    def parts_of(j, h=None):
        return [(j, q) for q in range(PARTS) if h is None or q // 4 == h]

    def arrived(ref, sem):
        pltpu.make_async_copy(ref, ref, sem).wait()

    weight_pass = pltpu.make_async_remote_copy(
        src_ref=weights, dst_ref=passed_weights, send_sem=weight_send, recv_sem=weight_recv,
        device_id=following, device_id_type=MESH,
    )

    start(pass_direct, pass_there, last, parts_of(0))
    prompt = [where for where in parts_of(0) if pass_routes[where] == last]
    relay_on(pass_there, pass_then, pass_routes, prompt)
    start(pass_direct, pass_there, last, parts_of(1))
    for copy in inputs:
        copy.wait()
    for i in range(2):
        weight = occupations[i].astype(jnp.float32) * (-0.5 * MIXING)
        weights[i] = jnp.full((8, N), weight, jnp.float32)
    weight_pass.start()

    def slab(index):
        return pl.ds(pl.multiple_of(index * SLAB, SLAB), SLAB)

    def half(h):
        return pl.ds(h * ROWS, ROWS)

    def half_of(index, h):
        return pl.ds(pl.multiple_of(index * SLAB + h * ROWS, ROWS), ROWS)

    def go(p, h):
        pltpu.make_async_copy(
            sent.at[p, slab(place), half(h)], middle.at[p, :, half_of(place, h)], go_recv.at[p]
        ).start()
        for peer in peers:
            pltpu.make_async_remote_copy(
                src_ref=sent.at[p, slab(peer), half(h)],
                dst_ref=middle.at[p, :, half_of(place, h)],
                send_sem=go_send.at[p], recv_sem=go_recv.at[p],
                device_id={"pw": peer}, device_id_type=MESH,
            ).start()

    def come(p, h):
        pltpu.make_async_copy(
            middle.at[p, :, half_of(place, h)], back.at[p, slab(place), half(h)],
            come_recv.at[p, h],
        ).start()
        for peer in peers:
            pltpu.make_async_remote_copy(
                src_ref=middle.at[p, :, half_of(peer, h)],
                dst_ref=back.at[p, slab(place), half(h)],
                send_sem=come_send.at[p], recv_sem=come_recv.at[p, h],
                device_id={"pw": peer}, device_id_type=MESH,
            ).start()

    def forward(i, j, p, h):
        @pl.loop(0, ROWS // 4)
        def _(quad):
            for r in range(2):
                at = pl.ds(h * ROWS + quad * 4 + r * 2, 2)
                field = (orbitals[i, at] * passing[j, at]).reshape(2 * N, N)
                field = from_right(field, table[0])
                field = from_left(table[1], side_by_side(field))
                turned[quad * 4 + r * 2] = field[:, :N]
                turned[quad * 4 + r * 2 + 1] = field[:, N:]

        @pl.loop(0, N // 16)
        def _(block):
            for b in range(2):
                rows = pl.ds(pl.multiple_of(block * 16 + b * 8, 8), 8)
                sent[p, rows, half(h)] = jnp.swapaxes(turned[:, rows], 0, 1)

    for j in range(2):
        for h in range(HALVES):
            arrived(passing.at[j, half(h)], pass_recv.at[j, h])
            for i in range(2):
                forward(i, j, 2 * j + i, h)
                go(2 * j + i, h)
        if j == 0:
            wave_x, share_x = wave_numbers(lax.broadcasted_iota(jnp.int32, (N, N), 0))
            wave_z, share_z = wave_numbers(lax.broadcasted_iota(jnp.int32, (N, N), 1))
            square_xz = wave_x + wave_z
            share_xz = share_x * share_z

            @pl.loop(0, SLAB)
            def _(y):
                wave_y, share_y = wave_numbers(
                    jnp.full((N, N), place * SLAB + y, jnp.int32)
                )
                square = square_xz + wave_y
                safe = jnp.where(square > 0, square, 1.0)
                factor = (4.0 * np.pi) * (share_xz * share_y)
                coulomb[y] = jnp.where(square > 0, factor / safe, 0.0)

    relay_on(
        pass_there, pass_then, pass_routes,
        [where for j in range(2) for where in parts_of(j) if where not in prompt],
    )

    core = lax.rem(band, 2)
    for p in range(4):
        arrived(middle.at[p], go_recv.at[p])
        signals = FIRST_TURNS.count(p)
        if signals:

            @pl.when(core == 0)
            def _():
                pl.semaphore_signal(turn, inc=signals, device_id=following, device_id_type=MESH)


        @pl.loop(0, SLAB // 4)
        def _(quad):
            for r in range(2):
                y = quad * 4 + r * 2
                field = jnp.concatenate([middle[p, y], middle[p, y + 1]], axis=1)
                field = from_left(table[1], field)
                field = field * jnp.concatenate([coulomb[y], coulomb[y + 1]], axis=1)
                field = from_left(table[2], field)
                middle[p, y] = field[:, :N]
                middle[p, y + 1] = field[:, N:]

        if FIRST_TURNS[p] is not None:

            @pl.when(core == 1)
            def _():
                pl.semaphore_wait(turn, 1)

        come(p, 0)


    @pl.when(core == 0)
    def _():
        for p in range(4):
            come(p, 1)

    for p in range(4):
        if TURNS[p] is None:
            pl.when(core == 1)(functools.partial(come, p, 1))

    weight_pass.wait_recv()
    for h in range(HALVES):
        for j in range(2):
            for i in range(2):
                p = 2 * j + i
                if (h, p) == (1, 2):
                    relay_on(term_there, term_then, term_routes, parts_of(0, 0) + parts_of(1, 0))
                for late in range(4):
                    if TURNS[late] == (h, p):

                        @pl.when(core == 1)
                        def _():
                            pl.semaphore_wait(turn, 1)
                            come(late, 1)

                arrived(back.at[p, :, half(h)], come_recv.at[p, h])
                for late in range(4):
                    if TURNS[late] == (h, p):

                        @pl.when(core == 0)
                        def _():
                            pl.semaphore_signal(
                                turn, inc=1, device_id=following, device_id_type=MESH
                            )


                @pl.loop(0, N // 16)
                def _(block):
                    for b in range(2):
                        rows = pl.ds(pl.multiple_of(block * 16 + b * 8, 8), 8)
                        turned[:, rows] = jnp.swapaxes(back[p, rows, half(h)], 0, 1)

                def backward(quad):
                    for r in range(2):
                        y = quad * 4 + r * 2
                        field = jnp.concatenate([turned[y], turned[y + 1]], axis=1)
                        field = from_left(table[2], field)
                        field = from_right(stacked(field), table[3])
                        potential = field.reshape(2, N // 8, 8, N)
                        at = pl.ds(h * ROWS + y, 2)
                        mine = (
                            potential * passing[j, at].reshape(2, N // 8, 8, N) * passed_weights[j]
                        ).reshape(2, N, N)
                        other = (
                            potential * orbitals[i, at].reshape(2, N // 8, 8, N) * weights[i]
                        ).reshape(2, N, N)
                        if j == 0:
                            out[i, at] = mine
                        else:
                            out[i, at] += mine
                        if i == 0:
                            theirs[j, at] = other
                        else:
                            theirs[j, at] += other

                if i == 0:
                    pl.loop(0, ROWS // 4)(backward)
                else:
                    for quad in range(ROWS // 4):
                        backward(quad)
                        q = 4 * h + 2 * quad
                        start(term_direct, term_there, first, [(j, q), (j, q + 1)])

    relay_on(term_there, term_then, term_routes, parts_of(0, 1) + parts_of(1, 1))
    for h in range(HALVES):
        for j in range(2):
            arrived(returned.at[j, half(h)], term_recv.at[j, h])

            @pl.loop(0, ROWS)
            def _(row):
                out[j, h * ROWS + row] += returned[j, h * ROWS + row]

    relay_end(pass_then, pass_routes)
    relay_end(term_then, term_routes)
    weight_pass.wait_send()
    for j in range(2):
        arrived(passing.at[j], pass_send.at[j])
        arrived(theirs.at[j], term_send.at[j])
    for p in range(4):
        others = pl.ds(0, N - SLAB)
        arrived(sent.at[p, others], go_send.at[p])
        arrived(back.at[p, others], come_send.at[p])


def shards(orbitals, occupations):
    vmem = pl.BlockSpec(memory_space=pltpu.VMEM)
    dma = pltpu.SemaphoreType.DMA
    hbm = pl.BlockSpec(memory_space=pltpu.HBM)
    return pl.pallas_call(
        kernel,
        out_shape=jax.ShapeDtypeStruct(orbitals.shape, jnp.float32),
        in_specs=[hbm, hbm, hbm],
        out_specs=vmem,
        scratch_shapes=[
            pltpu.SMEM(occupations.shape, jnp.int32),
            pltpu.VMEM(orbitals.shape, jnp.float32),
            pltpu.VMEM((4, 2 * N, 2 * N), jnp.bfloat16),
            pltpu.VMEM(orbitals.shape, jnp.float32),
            pltpu.VMEM((2, 8, N), jnp.float32),
            pltpu.VMEM((2, 8, N), jnp.float32),
            pltpu.VMEM((4, N, SLAB, N), jnp.float32),
            pltpu.VMEM((4, SLAB, N, N), jnp.float32),
            pltpu.VMEM((4, N, SLAB, N), jnp.float32),
            pltpu.VMEM(orbitals.shape, jnp.float32),
            pltpu.VMEM(orbitals.shape, jnp.float32),
            pltpu.VMEM((SLAB, N, N), jnp.float32),
            pltpu.VMEM((ROWS, N, N), jnp.float32),
            pltpu.VMEM((PARTS, PART, N, N), jnp.float32),
            pltpu.VMEM((PARTS, PART, N, N), jnp.float32),
            dma((3,)), dma((2,)), dma((2, HALVES)), dma, dma, dma((4,)), dma((4,)), dma((4,)),
            dma((4, HALVES)), dma((2,)), dma((2, HALVES)), dma((2, PARTS)), dma((2, PARTS)),
            pltpu.SemaphoreType.REGULAR,
        ],
        compiler_params=pltpu.CompilerParams(
            collective_id=0, has_side_effects=True, vmem_limit_bytes=48 * 1024 * 1024
        ),
        name="exchange",
    )(*(
        pltpu.with_memory_space_constraint(operand, pltpu.HBM)
        for operand in (occupations, orbitals, jnp.asarray(tables()))
    ))


def solution(mesh):
    placed = (P("band", "pw", None, None), P("band"))
    return jax.shard_map(
        shards, mesh=mesh, in_specs=placed, out_specs=P("band", "pw", None, None), check_vma=False
    )
```

```python
import functools

import jax
import jax.numpy as jnp
import numpy as np
from jax import lax
from jax.experimental import pallas as pl
from jax.experimental.pallas import tpu as pltpu
from jax.sharding import PartitionSpec as P

MIXING = 0.25
N = 128
HALF = N // 2
SLAB = 16
HALVES = 2
ROWS = SLAB // HALVES
MESH = pl.DeviceIdType.MESH
FAR_FIRST = ((2, 1), (1, 0), (3, 0), (0, 1), (2, 0), (1, 1), (3, 1))
PARTS = 8
FIRST_TURNS = (None, None, None, 2)
TURNS = ((0, 3), (1, 0), (1, 1), (1, 2))
PART = SLAB // PARTS


def tables():
    grid = np.arange(N)
    cosines = [np.cos(2.0 * np.pi * (k * grid % N) / N) for k in range(HALF + 1)]
    sines = [np.sin(2.0 * np.pi * (k * grid % N) / N) for k in range(1, HALF)]
    table = np.stack(cosines + sines, axis=1).astype(np.float32)
    high = table.astype(jnp.bfloat16)
    low = (table - high.astype(np.float32)).astype(jnp.bfloat16)
    right_forward = np.block([[high, low], [high, low]])
    left_forward = np.block([[high.T, high.T], [low.T, low.T]])
    left_inverse = np.block([[high, high], [low, low]])
    right_inverse = np.block([[high.T, low.T], [high.T, low.T]])
    return np.stack([right_forward, left_forward, left_inverse, right_inverse])


def split(value):
    high = value.astype(jnp.bfloat16)
    low = (value - high.astype(jnp.float32)).astype(jnp.bfloat16)
    return high, low


def from_right(value, table):
    high, low = split(value)
    both = jnp.dot(
        jnp.concatenate([high, low], axis=1), table, preferred_element_type=jnp.float32
    )
    return both[:, :N] + both[:, N:]


def from_left(table, value):
    high, low = split(value)
    both = jnp.dot(
        table, jnp.concatenate([high, low], axis=0), preferred_element_type=jnp.float32
    )
    return both[:N] + both[N:]


def side_by_side(value):
    return jnp.concatenate([value[:N], value[N:]], axis=1)


def stacked(value):
    return jnp.concatenate([value[:, :N], value[:, N:]], axis=0)


def wave_numbers(index):
    wave = jnp.where(index > HALF, index - HALF, index)
    share = jnp.where((wave == 0) | (wave == HALF), 1.0 / N, 2.0 / N)
    wave = wave.astype(jnp.float32) * (2.0 * np.pi / N)
    return wave * wave, share


def kernel(
    occupations_in, orbitals_in, table_in, out, occupations, orbitals, table, passing, weights,
    passed_weights, sent, middle, back, theirs, returned, coulomb, turned, pass_relay, term_relay,
    input_sem, pass_send, pass_recv, weight_send, weight_recv, go_send, go_recv, come_send,
    come_recv, term_send, term_recv, relay_send, relay_recv, turn,
):
    inputs = [
        pltpu.make_async_copy(orbitals_in, orbitals, input_sem.at[0]),
        pltpu.make_async_copy(table_in, table, input_sem.at[1]),
        pltpu.make_async_copy(occupations_in, occupations, input_sem.at[2]),
    ]
    for copy in inputs:
        copy.start()
    band = lax.axis_index("band")
    place = lax.axis_index("pw")
    bands = lax.axis_size("band")
    ring = bands // 2
    spot, base = lax.rem(band, ring), (band // ring) * ring
    across = lax.rem(base + ring, bands)
    following = {"band": lax.rem(band + 1, bands)}
    previous = {"band": lax.rem(band + bands - 1, bands)}
    place_x, place_y = lax.rem(place, 4), lax.div(place, 4)
    peers = [
        lax.rem(place_y + dy, 2) * 4 + lax.rem(place_x + dx, 4) for dx, dy in FAR_FIRST
    ]
    first, last = 0, ring - 1
    near_pass, near_term = (None, last, None, last, None, last, 7, 7), (None, first + 1) * 4
    far_pass = (3, 3, 5, 7, 3, ring - 3, 5, 7)
    far_term = (ring - 3, ring - 5, ring - 7, ring - 5)
    late_term = ((first + 1, ring - 7, first + 1, None), (first + 1, first + 1, None, None))
    pass_routes = {(j, q): (near_pass, far_pass)[j][q] for j in range(2) for q in range(PARTS)}
    term_routes = {
        (j, q): (far_term + late_term[j])[q] for j in range(2) for q in range(PARTS)
    }
    pass_relays = sorted({relay for relay in pass_routes.values() if relay is not None})
    term_relays = sorted({relay for relay in term_routes.values() if relay is not None})

    greetings = {}
    for here, there, far in (
        [(last, relay, True) for relay in pass_relays]
        + [(first, relay, False) for relay in pass_relays]
        + [(first, relay, True) for relay in term_relays]
        + [(last, relay, False) for relay in term_relays]
    ):
        greetings.setdefault(here, []).append((there, far))
        if here != there:
            greetings.setdefault(there, []).append((here, far))

    barrier = pltpu.get_barrier_semaphore()

    def greet(device):
        pl.semaphore_signal(barrier, inc=1, device_id=device, device_id_type=MESH)

    for device in [following, previous] + [{"pw": peer} for peer in peers]:
        greet(device)
    callers = 2 + len(peers)
    for here, others in greetings.items():
        callers = callers + len(others) * (spot == here).astype(jnp.int32)

        @pl.when(spot == here)
        def _():
            for other, far in others:
                greet({"band": (across if far else base) + other})

    pl.semaphore_wait(barrier, callers)

    def part(q):
        return pl.ds(q * PART, PART)

    def routes(source, target, relay, send, recv, relay_sends, relay_recvs, onward, ways, end):
        direct, there, then, taken = {}, {}, {}, {}
        for j in range(2):
            for q in range(PARTS):
                direct[j, q] = pltpu.make_async_remote_copy(
                    src_ref=source.at[j, part(q)], dst_ref=target.at[j, part(q)],
                    send_sem=send.at[j], recv_sem=recv.at[j, q // 4],
                    device_id=onward, device_id_type=MESH,
                )
                spot_of = ways[j, q]
                if spot_of is None:
                    continue
                slot = taken.get(spot_of, 0)
                taken[spot_of] = slot + 1
                there[j, q] = pltpu.make_async_remote_copy(
                    src_ref=source.at[j, part(q)], dst_ref=relay.at[slot],
                    send_sem=send.at[j], recv_sem=relay_recvs.at[slot],
                    device_id={"band": across + spot_of}, device_id_type=MESH,
                )
                then[j, q] = pltpu.make_async_remote_copy(
                    src_ref=relay.at[slot], dst_ref=target.at[j, part(q)],
                    send_sem=relay_sends.at[slot], recv_sem=recv.at[j, q // 4],
                    device_id={"band": base + end}, device_id_type=MESH,
                )
        return direct, there, then

    pass_direct, pass_there, pass_then = routes(
        orbitals_in, passing, pass_relay, pass_send, pass_recv,
        relay_send.at[0], relay_recv.at[0], following, pass_routes, first,
    )
    term_direct, term_there, term_then = routes(
        theirs, returned, term_relay, term_send, term_recv,
        relay_send.at[1], relay_recv.at[1], previous, term_routes, last,
    )

    def start(direct, there, source, parts):
        @pl.when(spot == source)
        def _():
            for where in parts:
                there.get(where, direct[where]).start()

        @pl.when(spot != source)
        def _():
            for where in parts:
                direct[where].start()

    def relay_on(there, then, ways, parts):
        for relay in sorted({ways[where] for where in parts if where in then}):

            @pl.when(spot == relay)
            def _():
                for where in parts:
                    if ways[where] == relay:
                        there[where].wait_recv()
                        then[where].start()

    def relay_end(then, ways):
        for relay in sorted({ways[where] for where in then}):

            @pl.when(spot == relay)
            def _():
                for where, copy in then.items():
                    if ways[where] == relay:
                        copy.wait_send()

    def parts_of(j, h=None):
        return [(j, q) for q in range(PARTS) if h is None or q // 4 == h]

    def arrived(ref, sem):
        pltpu.make_async_copy(ref, ref, sem).wait()

    weight_pass = pltpu.make_async_remote_copy(
        src_ref=weights, dst_ref=passed_weights, send_sem=weight_send, recv_sem=weight_recv,
        device_id=following, device_id_type=MESH,
    )

    start(pass_direct, pass_there, last, parts_of(0))
    prompt = [where for where in parts_of(0) if pass_routes[where] == last]
    relay_on(pass_there, pass_then, pass_routes, prompt)
    start(pass_direct, pass_there, last, parts_of(1))
    for copy in inputs:
        copy.wait()
    for i in range(2):
        weight = occupations[i].astype(jnp.float32) * (-0.5 * MIXING)
        weights[i] = jnp.full((8, N), weight, jnp.float32)
    weight_pass.start()

    def slab(index):
        return pl.ds(pl.multiple_of(index * SLAB, SLAB), SLAB)

    def half(h):
        return pl.ds(h * ROWS, ROWS)

    def half_of(index, h):
        return pl.ds(pl.multiple_of(index * SLAB + h * ROWS, ROWS), ROWS)

    def go(p, h):
        pltpu.make_async_copy(
            sent.at[p, slab(place), half(h)], middle.at[p, :, half_of(place, h)], go_recv.at[p]
        ).start()
        for peer in peers:
            pltpu.make_async_remote_copy(
                src_ref=sent.at[p, slab(peer), half(h)],
                dst_ref=middle.at[p, :, half_of(place, h)],
                send_sem=go_send.at[p], recv_sem=go_recv.at[p],
                device_id={"pw": peer}, device_id_type=MESH,
            ).start()

    def come(p, h):
        pltpu.make_async_copy(
            middle.at[p, :, half_of(place, h)], back.at[p, slab(place), half(h)],
            come_recv.at[p, h],
        ).start()
        for peer in peers:
            pltpu.make_async_remote_copy(
                src_ref=middle.at[p, :, half_of(peer, h)],
                dst_ref=back.at[p, slab(place), half(h)],
                send_sem=come_send.at[p], recv_sem=come_recv.at[p, h],
                device_id={"pw": peer}, device_id_type=MESH,
            ).start()

    def forward(i, j, p, h):
        @pl.loop(0, ROWS // 4)
        def _(quad):
            for r in range(2):
                at = pl.ds(h * ROWS + quad * 4 + r * 2, 2)
                field = (orbitals[i, at] * passing[j, at]).reshape(2 * N, N)
                field = from_right(field, table[0])
                field = from_left(table[1], side_by_side(field))
                turned[quad * 4 + r * 2] = field[:, :N]
                turned[quad * 4 + r * 2 + 1] = field[:, N:]

        @pl.loop(0, N // 16)
        def _(block):
            for b in range(2):
                rows = pl.ds(pl.multiple_of(block * 16 + b * 8, 8), 8)
                sent[p, rows, half(h)] = jnp.swapaxes(turned[:, rows], 0, 1)

    for j in range(2):
        for h in range(HALVES):
            arrived(passing.at[j, half(h)], pass_recv.at[j, h])
            for i in range(2):
                forward(i, j, 2 * j + i, h)
                go(2 * j + i, h)
        if j == 0:
            wave_x, share_x = wave_numbers(lax.broadcasted_iota(jnp.int32, (N, N), 0))
            wave_z, share_z = wave_numbers(lax.broadcasted_iota(jnp.int32, (N, N), 1))
            square_xz = wave_x + wave_z
            share_xz = share_x * share_z

            @pl.loop(0, SLAB)
            def _(y):
                wave_y, share_y = wave_numbers(
                    jnp.full((N, N), place * SLAB + y, jnp.int32)
                )
                square = square_xz + wave_y
                safe = jnp.where(square > 0, square, 1.0)
                factor = (4.0 * np.pi) * (share_xz * share_y)
                coulomb[y] = jnp.where(square > 0, factor / safe, 0.0)

    relay_on(
        pass_there, pass_then, pass_routes,
        [where for j in range(2) for where in parts_of(j) if where not in prompt],
    )

    core = lax.rem(band, 2)
    for p in range(4):
        arrived(middle.at[p], go_recv.at[p])
        signals = FIRST_TURNS.count(p)
        if signals:

            @pl.when(core == 0)
            def _():
                pl.semaphore_signal(turn, inc=signals, device_id=following, device_id_type=MESH)


        @pl.loop(0, SLAB // 4)
        def _(quad):
            for r in range(2):
                y = quad * 4 + r * 2
                field = jnp.concatenate([middle[p, y], middle[p, y + 1]], axis=1)
                field = from_left(table[1], field)
                field = field * jnp.concatenate([coulomb[y], coulomb[y + 1]], axis=1)
                field = from_left(table[2], field)
                middle[p, y] = field[:, :N]
                middle[p, y + 1] = field[:, N:]

        if FIRST_TURNS[p] is not None:

            @pl.when(core == 1)
            def _():
                pl.semaphore_wait(turn, 1)

        come(p, 0)


    @pl.when(core == 0)
    def _():
        for p in range(4):
            come(p, 1)

    for p in range(4):
        if TURNS[p] is None:
            pl.when(core == 1)(functools.partial(come, p, 1))

    weight_pass.wait_recv()
    for h in range(HALVES):
        for j in range(2):
            for i in range(2):
                p = 2 * j + i
                if (h, p) == (1, 2):
                    relay_on(term_there, term_then, term_routes, parts_of(0, 0) + parts_of(1, 0))
                for late in range(4):
                    if TURNS[late] == (h, p):

                        @pl.when(core == 1)
                        def _():
                            pl.semaphore_wait(turn, 1)
                            come(late, 1)

                arrived(back.at[p, :, half(h)], come_recv.at[p, h])
                for late in range(4):
                    if TURNS[late] == (h, p):

                        @pl.when(core == 0)
                        def _():
                            pl.semaphore_signal(
                                turn, inc=1, device_id=following, device_id_type=MESH
                            )


                @pl.loop(0, N // 16)
                def _(block):
                    for b in range(2):
                        rows = pl.ds(pl.multiple_of(block * 16 + b * 8, 8), 8)
                        turned[:, rows] = jnp.swapaxes(back[p, rows, half(h)], 0, 1)

                def backward(quad):
                    for r in range(2):
                        y = quad * 4 + r * 2
                        field = jnp.concatenate([turned[y], turned[y + 1]], axis=1)
                        field = from_left(table[2], field)
                        field = from_right(stacked(field), table[3])
                        potential = field.reshape(2, N // 8, 8, N)
                        at = pl.ds(h * ROWS + y, 2)
                        mine = (
                            potential * passing[j, at].reshape(2, N // 8, 8, N) * passed_weights[j]
                        ).reshape(2, N, N)
                        other = (
                            potential * orbitals[i, at].reshape(2, N // 8, 8, N) * weights[i]
                        ).reshape(2, N, N)
                        if j == 0:
                            out[i, at] = mine
                        else:
                            out[i, at] += mine
                        if i == 0:
                            theirs[j, at] = other
                        else:
                            theirs[j, at] += other

                if i == 0:
                    pl.loop(0, ROWS // 4)(backward)
                else:
                    for quad in range(ROWS // 4):
                        backward(quad)
                        q = 4 * h + 2 * quad
                        start(term_direct, term_there, first, [(j, q), (j, q + 1)])

    relay_on(term_there, term_then, term_routes, parts_of(0, 1) + parts_of(1, 1))
    for h in range(HALVES):
        for j in range(2):
            arrived(returned.at[j, half(h)], term_recv.at[j, h])

            @pl.loop(0, ROWS)
            def _(row):
                out[j, h * ROWS + row] += returned[j, h * ROWS + row]

    relay_end(pass_then, pass_routes)
    relay_end(term_then, term_routes)
    weight_pass.wait_send()
    for j in range(2):
        arrived(passing.at[j], pass_send.at[j])
        arrived(theirs.at[j], term_send.at[j])
    for p in range(4):
        others = pl.ds(0, N - SLAB)
        arrived(sent.at[p, others], go_send.at[p])
        arrived(back.at[p, others], come_send.at[p])


def shards(orbitals, occupations):
    vmem = pl.BlockSpec(memory_space=pltpu.VMEM)
    dma = pltpu.SemaphoreType.DMA
    hbm = pl.BlockSpec(memory_space=pltpu.HBM)
    return pl.pallas_call(
        kernel,
        out_shape=jax.ShapeDtypeStruct(orbitals.shape, jnp.float32),
        in_specs=[hbm, hbm, hbm],
        out_specs=vmem,
        scratch_shapes=[
            pltpu.SMEM(occupations.shape, jnp.int32),
            pltpu.VMEM(orbitals.shape, jnp.float32),
            pltpu.VMEM((4, 2 * N, 2 * N), jnp.bfloat16),
            pltpu.VMEM(orbitals.shape, jnp.float32),
            pltpu.VMEM((2, 8, N), jnp.float32),
            pltpu.VMEM((2, 8, N), jnp.float32),
            pltpu.VMEM((4, N, SLAB, N), jnp.float32),
            pltpu.VMEM((4, SLAB, N, N), jnp.float32),
            pltpu.VMEM((4, N, SLAB, N), jnp.float32),
            pltpu.VMEM(orbitals.shape, jnp.float32),
            pltpu.VMEM(orbitals.shape, jnp.float32),
            pltpu.VMEM((SLAB, N, N), jnp.float32),
            pltpu.VMEM((ROWS, N, N), jnp.float32),
            pltpu.VMEM((PARTS, PART, N, N), jnp.float32),
            pltpu.VMEM((PARTS, PART, N, N), jnp.float32),
            dma((3,)), dma((2,)), dma((2, HALVES)), dma, dma, dma((4,)), dma((4,)), dma((4,)),
            dma((4, HALVES)), dma((2,)), dma((2, HALVES)), dma((2, PARTS)), dma((2, PARTS)),
            pltpu.SemaphoreType.REGULAR,
        ],
        compiler_params=pltpu.CompilerParams(
            collective_id=0, has_side_effects=True, vmem_limit_bytes=48 * 1024 * 1024
        ),
        name="exchange",
    )(*(
        pltpu.with_memory_space_constraint(operand, pltpu.HBM)
        for operand in (occupations, orbitals, jnp.asarray(tables()))
    ))


def solution(mesh):
    placed = (P("band", "pw", None, None), P("band"))
    return jax.shard_map(
        shards, mesh=mesh, in_specs=placed, out_specs=P("band", "pw", None, None), check_vma=False
    )
```
